256 devices in a mesh: section: 4 (over x), replica: 64 (over z, y, core).
Axes of the slice: x: 4, y: 4, z: 8, core: 2. Of those that a mesh axis runs over, the one named last changes fastest.
Arguments:
- tokens: bfloat16 [4, 64, 2560], P(None, 'replica'), may hold values from -6 to 6
- cotangent: bfloat16 [4, 64, 2560], P(None, 'replica'), may hold values from -6 to 6
- wiring: int32 [4, 4, 1], replicated, may hold values from 0 to 3; in each aligned block of 4 rows (0 to 3, 4 to 7, ..., all dimensions but the last counted through in order) at most 2 rows name the same one
- lengths: int32 [4], replicated, may hold values from 16 to 64, as said below
- in_proj: bfloat16 [4, 64, 2560, 640], P('section', 'replica'), may hold values from -0.125 to 0.125
- out_proj: bfloat16 [4, 64, 2560, 640], P('section', 'replica'), may hold values from -0.0625 to 0.0625
- section_gain: bfloat16 [4, 4, 2560], P('section'), may hold values from 0.099609375 to 1.8984375
Outputs:
- input_grad: bfloat16 [4, 64, 2560], P('section', 'replica')
- in_grad: bfloat16 [4, 2560, 10240], P('section', None, 'replica')
- out_grad: bfloat16 [4, 2560, 10240], P('section', None, 'replica')
The draws below stay inside these ranges and needn't reach their ends.
Inputs may be any that keep to these rules, and one draw needn't show every extreme that they name: wiring[t, i, 0] is the replica of section t that processes micro-batch i; at every section no replica is named by more than 2 micro-batches, and at some section one is named by exactly 2. `lengths`: some micro-batch has exactly 64 live tokens and some exactly 16.
All inputs are finite; a program needn't handle non-finite values.
Results may differ from the reference program's by a relative error of at most 0.027.
Values may be sent and summed in bfloat16 or wider, within the bound.
A program may use at most 128 MiB of HBM per device.

```python
import math
import jax
import jax.numpy as jnp
import numpy as np
from jax import lax

D = 2560
FF_DEV = 640
GROUPS = 4
CAP = 2
MICRO = 4
TOK = 64
FF = 10240
N_SECTION = 4
N_REPLICA = 64


def draw_lengths(key, part):
    key = jax.random.fold_in(key, 7)
    key_values, key_spots = jax.random.split(key)
    values = jax.random.randint(key_values, (MICRO,), TOK // 4, TOK + 1)
    picked = jax.random.permutation(key_spots, MICRO)
    values = values.at[picked[0]].set(TOK)
    values = values.at[picked[1]].set(TOK // 4)
    return values.astype(jnp.int32)


def levels(rng, extent, shards, least, high):
    gain, own = 1.0, jax.random.fold_in(rng, 6)
    for dim, shards_of in shards:
        heights = jnp.exp(jax.random.uniform(jax.random.fold_in(own, dim), (shards_of,), jnp.float32, least / len(shards), high / len(shards)))
        gain = gain * jnp.repeat(heights, extent[dim] // shards_of).reshape([-1 if axis == dim else 1 for axis in range(len(extent))])
    return gain


def deal_out(own_key, own, number, rows, amount, top, bound, slope):
    order = jax.random.permutation(own_key, amount)
    packed, ordinary = portions_of(amount, rows * top, bound, slope, True), portions_of(amount, rows * top, bound, slope, False)
    places = jnp.arange(amount)

    def named(sizes, rotation):
        used = int((sizes > 0).sum())
        fixed = max(1, used // 4)
        passed = fixed + (places - fixed + rotation * (used - fixed)) % max(1, amount - fixed)
        return jnp.zeros((amount,), jnp.int32).at[order[jnp.where(places < fixed, places, passed)]].set(jnp.asarray(sizes, jnp.int32))

    sizes = jnp.where(number % 4 == 0, named(packed, number // 4), named(ordinary, number - number // 4 - 1))
    mixed = jax.random.permutation(jax.random.fold_in(own, 3), amount)
    source_of, sink = mixed[0:amount // 2 * 2:2], mixed[1:amount // 2 * 2:2]
    margin = jnp.minimum(sizes[source_of] - 1, bound - sizes[sink]) // 2
    margin = jnp.where((source_of == order[0]) | (sink == order[0]) | (sizes[sink] == 0), 0, jnp.maximum(margin, 0))
    passed = jax.random.randint(jax.random.fold_in(own, 4), (amount // 2,), 0, 1 << 20) % (margin + 1)
    sizes = sizes.at[source_of].add(-passed).at[sink].add(passed)
    members = jnp.searchsorted(jnp.cumsum(sizes), jnp.arange(rows * top), side="right").astype(jnp.int32)
    table = members.reshape(top, rows).T
    table = table[jax.random.permutation(jax.random.fold_in(own, 1), rows)]
    rotation = jax.random.randint(jax.random.fold_in(own, 2), (rows, 1), 0, top)
    return jnp.take_along_axis(table, (jnp.arange(top)[None, :] + rotation) % top, axis=1)


def portions_of(count, total, limit, slope, full):
    portions = [(1 << 20) // math.isqrt(grade ** slope) + 1 for grade in range(1, count + 1)]
    largest = limit if full else min(limit, max(-(-total // count), total * portions[0] // sum(portions)))
    least = 1 if total - largest >= count - 1 else 0
    counts, surplus = [largest] + [least] * (count - 1), total - largest - least * (count - 1)
    while surplus > 0:
        candidates = [i for i in range(1, count) if counts[i] < largest] or [i for i in range(1, count) if counts[i] < limit]
        whole, budget = sum([portions[i] for i in candidates]), surplus
        for i in candidates:
            addition = min(limit - counts[i], max(1, budget * portions[i] // whole), surplus)
            counts[i] = counts[i] + addition
            surplus = surplus - addition
    return np.array(counts)


def bell_draw(rng, dims, scale, limit, shards=(), held_as=jnp.bfloat16):
    result = jax.random.normal(rng, dims, jnp.float32) * scale
    if len(shards) > 0:
        result = levels(rng, dims, shards, -0.22, 0.18) * result
    return jnp.clip(result, min=-limit, max=limit).astype(held_as)


def setup_inputs(seed: int = 0) -> dict:
    keys = jax.random.split(jax.random.key(seed), 8)
    tokens = bell_draw(keys[0], (MICRO, TOK, D), 1.0, 6.0, ((1, 64),))
    cotangent = bell_draw(keys[1], (MICRO, TOK, D), 1.0, 6.0, ((1, 64),))
    wiring_keys = jax.random.split(jax.random.fold_in(keys[2], 1), N_SECTION * MICRO // MICRO)
    wiring_turns = jax.random.permutation(jax.random.fold_in(keys[2], 3), N_SECTION * MICRO // MICRO)
    wiring = jax.vmap(lambda own, number: deal_out(jax.random.fold_in(keys[2], 2), own, number, MICRO, GROUPS, 1, CAP, 2))(wiring_keys, wiring_turns).reshape((N_SECTION, MICRO, 1))
    lengths = draw_lengths(jax.random.fold_in(keys[7], 71), 0)
    in_proj = bell_draw(keys[4], (N_SECTION, N_REPLICA, D, FF_DEV), D ** -0.5, 0.125, ((0, 4), (1, 64)))
    out_proj = bell_draw(keys[5], (N_SECTION, N_REPLICA, D, FF_DEV), FF ** -0.5, 0.0625, ((0, 4), (1, 64)))
    section_gain = jnp.clip(1.0 + 0.18 * jax.random.normal(keys[6], (N_SECTION, GROUPS, D), jnp.float32), 0.099609375, 1.8984375).astype(jnp.bfloat16)
    return dict(tokens=tokens, cotangent=cotangent, wiring=wiring, lengths=lengths, in_proj=in_proj, out_proj=out_proj, section_gain=section_gain)


gelu_coeff = 0.7978845608028654
gelu_cubic = 0.044715
epsilon = 1e-05

def full_weights(stack):
    span_count = stack.shape[0] // GROUPS
    feature = stack.shape[1]
    hidden_units = stack.shape[2]
    return stack.reshape(span_count, GROUPS, feature, hidden_units).transpose(1, 2, 0, 3).reshape(GROUPS, feature, span_count * hidden_units)

def norm_rows(rows, gain_vec):
    flattened = rows.astype(jnp.float32)
    inv_rms = lax.rsqrt(lax.optimization_barrier(jnp.mean(flattened * flattened, axis=-1, keepdims=True)) + epsilon)
    normed = (flattened * inv_rms * gain_vec.astype(jnp.float32)).astype(jnp.bfloat16)
    return (flattened, inv_rms, normed)

def section_forward(rows, row_mask, w_in, w_out, gain_vec):
    flattened, inv_rms, normed = norm_rows(rows, gain_vec)
    pre_act = jnp.dot(normed, w_in, preferred_element_type=jnp.float32)
    activated = jax.nn.gelu(pre_act, approximate=True).astype(jnp.bfloat16)
    branch = lax.dot_general(activated, w_out, (((1,), (1,)), ((), ())), preferred_element_type=jnp.float32)
    return (flattened + row_mask[:, None] * branch).astype(jnp.bfloat16)

def section_backward(rows, incoming, row_mask, w_in, w_out, gain_vec):
    flattened, inv_rms, normed = norm_rows(rows, gain_vec)
    pre_act = jnp.dot(normed, w_in, preferred_element_type=jnp.float32)
    activated = jax.nn.gelu(pre_act, approximate=True).astype(jnp.bfloat16)
    masked = (incoming.astype(jnp.float32) * row_mask[:, None]).astype(jnp.bfloat16)
    out_part = lax.dot_general(masked, activated, (((0,), (0,)), ((), ())), preferred_element_type=jnp.float32)
    act_grad = jnp.dot(masked, w_out, preferred_element_type=jnp.float32)
    inner_arg = gelu_coeff * (pre_act + gelu_cubic * pre_act * pre_act * pre_act)
    tangent = jnp.tanh(inner_arg)
    derivative = 0.5 * (1.0 + tangent) + 0.5 * pre_act * (1.0 - tangent * tangent) * gelu_coeff * (1.0 + 3.0 * gelu_cubic * pre_act * pre_act)
    pre_grad = (act_grad * derivative).astype(jnp.bfloat16)
    in_part = lax.dot_general(normed, pre_grad, (((0,), (0,)), ((), ())), preferred_element_type=jnp.float32)
    norm_grad = lax.dot_general(pre_grad, w_in, (((1,), (1,)), ((), ())), preferred_element_type=jnp.float32)
    pulled = norm_grad * gain_vec.astype(jnp.float32)[None, :]
    hidden_grad = incoming.astype(jnp.float32) + inv_rms * pulled - flattened * inv_rms * inv_rms * inv_rms * lax.optimization_barrier(jnp.mean(flattened * pulled, axis=1, keepdims=True))
    return (hidden_grad.astype(jnp.bfloat16), in_part, out_part)

def reference(tokens, cotangent, wiring, lengths, in_proj, out_proj, section_gain):
    routes = wiring[:, :, 0]
    positions = jnp.arange(tokens.shape[1], dtype=jnp.int32)
    live_mask = (positions[None, :] < lengths[:, None]).astype(jnp.float32)
    hidden = tokens
    inputs = []
    for section_no in range(N_SECTION):
        inputs.append(hidden)
        if section_no + 1 < N_SECTION:
            w_in_all = full_weights(in_proj[section_no])
            w_out_all = full_weights(out_proj[section_no])

            def advance(record, w_in_all=w_in_all, w_out_all=w_out_all, section_no=section_no):
                sample, row_mask, replica_id = record
                return section_forward(sample, row_mask, w_in_all[replica_id], w_out_all[replica_id], section_gain[section_no, replica_id])
            hidden = lax.map(advance, (hidden, live_mask, routes[section_no]))
    upstream = cotangent
    in_parts = [None] * N_SECTION
    out_parts = [None] * N_SECTION
    for section_no in range(N_SECTION - 1, -1, -1):
        w_in_all = full_weights(in_proj[section_no])
        w_out_all = full_weights(out_proj[section_no])

        def retreat(totals, record, w_in_all=w_in_all, w_out_all=w_out_all, section_no=section_no):
            sample, incoming, row_mask, replica_id = record
            returned, grad_in, grad_out = section_backward(sample, incoming, row_mask, w_in_all[replica_id], w_out_all[replica_id], section_gain[section_no, replica_id])
            return ((totals[0] + grad_in, totals[1] + grad_out), returned)
        zeroes = jnp.zeros((w_in_all.shape[1], w_in_all.shape[2]), jnp.float32)
        (in_total, out_total), upstream = lax.scan(retreat, (zeroes, zeroes), (inputs[section_no], upstream, live_mask, routes[section_no]))
        in_parts[section_no] = in_total.astype(jnp.bfloat16)
        out_parts[section_no] = out_total.astype(jnp.bfloat16)
    return (upstream, jnp.stack(in_parts), jnp.stack(out_parts))
```

```python
import jax
import jax.numpy as jnp
from jax import lax
from jax.experimental import pallas as pl
from jax.experimental.pallas import tpu as pltpu
from jax.sharding import PartitionSpec as P

D = 2560
FF_DEV = 640
GROUPS = 4
CAP = 2
MICRO = 4
CHUNKS = 4
ROWS = 16
HALF = D // 2
QUART = D // 4
SLOT_ROWS = CAP * ROWS
PIECE = FF_DEV // GROUPS
CHIPS = 32

gelu_coeff = 0.7978845608028654
gelu_cubic = 0.044715
epsilon = 1e-05

BF = jnp.bfloat16
F32 = jnp.float32
NT = (((1,), (1,)), ((), ()))

SLOT_MB, SLOT_LEN, MERGE, GROUP_OF, PLACE_OF, LENGTH = 0, 2, 4, 8, 12, 16


def choose(index, values):
    picked = values[0]
    for n in range(1, len(values)):
        picked = jnp.where(index == n, values[n], picked)
    return picked


def norm_scale(rows):
    return lax.rsqrt(jnp.mean(rows * rows, axis=-1, keepdims=True) + epsilon)


def kernel(
    table, tokens, cotangent, w_in_hbm, w_out_hbm, gain_ref,
    normed_out, masked_out, pre_out, act_out, grad_out,
    x_buf, u_buf, w_in, w_out, gains,
    pre_buf, pg_stage, act_stage, pg_all, act_all,
    merge_send_f, merge_own_f, merge_recv_f, rs_send_f, rs_recv_f, own_f,
    merge_send_b, merge_own_b, merge_recv_b, rs_send_b, rs_recv_b, own_b, final_recv,
    load_sem, x_sem, x_core_sem, u_sem, u_core_sem, core_send_sem,
    merge_sem_f, merge_sem_b, merge_send_sem, rs_sem, rs_send_sem, ag_send_sem,
    grads_sem, grads_send_sem, final_sem, final_send_sem, local_sem,
):
    t = lax.axis_index("section")
    r = lax.axis_index("replica")
    core = lax.rem(r, 2)
    chip = lax.div(r, 2)
    z = lax.div(r, 8)
    y = lax.rem(chip, 4)
    g = lax.rem(r, 4)
    part = lax.div(r, 4)
    last = lax.axis_size("section") - 1
    own_k = 2 * core + lax.rem(y + z, 2)
    own_i = lax.div(part, 4)
    own_j = lax.rem(part, 4)
    own_cols = pl.ds(pl.multiple_of(own_j * QUART, 128), QUART)
    mate = r + 1 - 2 * core
    my_half = pl.ds(pl.multiple_of(core * HALF, 128), HALF)
    mate_rows = pl.ds(pl.multiple_of((1 - core) * HALF, HALF), HALF)
    my_rows = pl.ds(pl.multiple_of(core * HALF, HALF), HALF)

    def to(section, replica):
        return dict(device_id=(section, replica), device_id_type=pl.DeviceIdType.MESH)

    in_load = pltpu.make_async_copy(w_in_hbm, w_in, load_sem.at[0])
    out_load = pltpu.make_async_copy(w_out_hbm, w_out, load_sem.at[1])
    x_load = pltpu.make_async_copy(tokens, x_buf, load_sem.at[2])
    u_load = pltpu.make_async_copy(cotangent, u_buf, load_sem.at[3])

    @pl.when(t == 0)
    def _():
        x_load.start()

    in_load.start()
    out_load.start()

    @pl.when(t == last)
    def _():
        u_load.start()

    gains[...] = gain_ref[...].astype(F32)
    in_load.wait()
    out_load.wait()

    @pl.when(t == 0)
    def _():
        x_load.wait()

    @pl.when(t == last)
    def _():
        u_load.wait()

    def gain_row(group):
        return choose(group, [gains[n : n + 1, :] for n in range(GROUPS)])

    def core_copy(buf, k, sem):
        view = buf.at[k, :, :, my_half]
        return pltpu.make_async_remote_copy(view, view, core_send_sem.at[0], sem.at[k], **to(t, mate))

    def arrive(buf, k, sem, core_sem):
        view = buf.at[k, :, :, my_half]
        pltpu.make_async_copy(view, view, sem.at[k]).wait()
        copy = core_copy(buf, k, core_sem)
        copy.start()
        copy.wait()

    def slot_rows(buf, k):
        rows = [buf[k, i] for i in range(MICRO)]
        return [choose(table[SLOT_MB + c], rows) for c in range(CAP)]

    def enter(k):
        gain = gain_row(g)
        parts = []
        for rows in slot_rows(x_buf, k):
            flat = rows.astype(F32)
            parts.append((flat * norm_scale(flat) * gain).astype(BF))
        normed = jnp.concatenate(parts, axis=0)
        pre = jnp.dot(normed, w_in[...], preferred_element_type=F32)
        pre_buf[k] = pre
        act = jax.nn.gelu(pre, approximate=True).astype(BF)
        for n in range(GROUPS):
            act_stage[n, k] = act[:, n * PIECE : (n + 1) * PIECE]
        return act

    def owner_of(k, i, jj):
        oz = 2 * i + core
        oy = 2 * jj + lax.rem(oz + k, 2)
        return oz * 8 + oy * 2 + lax.div(k, 2)

    def merge_copy(k, send, recv, sem):
        return pltpu.make_async_remote_copy(
            send.at[k], recv.at[k], merge_send_sem.at[0], sem.at[k], **to(t, mate)
        )

    def piece_copy(k, i, jj, send, recv, way):
        target = owner_of(k, i, jj)
        return target, pltpu.make_async_remote_copy(
            send.at[k, i, jj], recv.at[chip], rs_send_sem.at[way], rs_sem.at[way], **to(t, target)
        )

    def scatter(k, hidden, weight, extra, send, own, recv, rs_send, rs_recv, sem, way):
        width = HALF if extra is None else HALF + 128
        theirs = lax.dot_general(hidden, weight[mate_rows, :], NT, preferred_element_type=F32)
        send[k, :, 0:HALF] = theirs.astype(BF)
        if extra is not None:
            send[k, :, HALF:width] = extra
        copy = merge_copy(k, send, recv, sem)
        copy.start()
        mine = lax.dot_general(hidden, weight[my_rows, :], NT, preferred_element_type=F32)
        own[:, 0:HALF] = mine.astype(BF)
        if extra is not None:
            own[:, HALF:width] = extra
        copy.wait()
        for i in range(MICRO):
            which = table[MERGE + i]
            zero = jnp.zeros((ROWS, width), BF)
            merged = choose(
                which,
                [own[0:ROWS, :], own[ROWS:SLOT_ROWS, :], recv[k, 0:ROWS, :], recv[k, ROWS:SLOT_ROWS, :], zero],
            )
            for jj in range(2):
                rs_send[k, i, jj, :, 0:QUART] = merged[:, jj * QUART : (jj + 1) * QUART]
                if extra is not None:
                    rs_send[k, i, jj, :, QUART : QUART + 128] = merged[:, HALF:width]

        def send_piece(n, carry):
            i, jj = lax.div(n, 2), lax.rem(n, 2)
            target, remote = piece_copy(k, i, jj, rs_send, rs_recv, way)

            @pl.when(target != r)
            def _():
                remote.start()

            @pl.when(target == r)
            def _():
                pltpu.make_async_copy(rs_send.at[k, i, jj], rs_recv.at[chip], rs_sem.at[way]).start()

            return carry

        lax.fori_loop(0, 2 * MICRO, send_piece, 0)

    def scatter_done(rs_send, rs_recv, way):
        def wait_piece(n, carry):
            k, m = lax.div(n, 2 * MICRO), lax.rem(n, 2 * MICRO)
            target, remote = piece_copy(k, lax.div(m, 2), lax.rem(m, 2), rs_send, rs_recv, way)

            @pl.when(target != r)
            def _():
                remote.wait_send()

            return carry

        lax.fori_loop(0, CHUNKS * 2 * MICRO, wait_piece, 0)

    def total(recv):
        return jnp.sum(recv[...].astype(F32), axis=0)

    def live_rows(k, length):
        position = k * ROWS + lax.broadcasted_iota(jnp.int32, (ROWS, 1), 0)
        return position < length

    def spread_copy(n, source, buf, section, sem, way):
        a, b = lax.div(n, 4), lax.rem(n, 4)
        dz = 4 + (2 * lax.rem(a, 2) - 1) * lax.div(a + 1, 2)
        dy = 2 + (2 * lax.rem(b, 2) - 1) * lax.div(b + 1, 2)
        target = lax.rem(z + dz, 8) * 8 + lax.rem(y + dy, 4) * 2 + lax.div(own_j, 2)
        return pltpu.make_async_remote_copy(
            source, buf.at[own_k, own_i, :, own_cols], ag_send_sem.at[way], sem.at[own_k], **to(section, target)
        )

    def spread(source, buf, section, sem, way):
        def one(n, carry):
            spread_copy(n, source, buf, section, sem, way).start()
            return carry

        lax.fori_loop(0, CHIPS, one, 0)

    def spread_done(source, buf, section, sem, way):
        def one(n, carry):
            spread_copy(n, source, buf, section, sem, way).wait_send()
            return carry

        lax.fori_loop(0, CHIPS, one, 0)

    @pl.when(t < last)
    def _():
        def step(k, carry):
            @pl.when(t > 0)
            def _():
                arrive(x_buf, k, x_sem, x_core_sem)

            act = enter(k)
            scatter(
                k, act, w_out, None, merge_send_f, merge_own_f, merge_recv_f,
                rs_send_f, rs_recv_f, merge_sem_f, 0,
            )
            return carry

        lax.fori_loop(0, CHUNKS, step, 0)
        pltpu.make_async_copy(rs_recv_f, rs_recv_f, rs_sem.at[0]).wait()
        branch = total(rs_recv_f)
        live = live_rows(own_k, table[LENGTH + own_i]).astype(F32)
        held = x_buf[own_k, own_i, :, own_cols].astype(F32)
        own_f[...] = (held + live * branch).astype(BF)
        spread(own_f, x_buf, t + 1, x_sem, 0)

    def back(k, carry):
        @pl.when(t == last)
        def _():
            arrive(x_buf, k, x_sem, x_core_sem)
            enter(k)

        @pl.when(t < last)
        def _():
            arrive(u_buf, k, u_sem, u_core_sem)

        parts = []
        for c, rows in enumerate(slot_rows(u_buf, k)):
            live = live_rows(k, table[SLOT_LEN + c]).astype(F32)
            parts.append((rows.astype(F32) * live).astype(BF))
        masked = jnp.concatenate(parts, axis=0)
        act_grad = jnp.dot(masked, w_out[...], preferred_element_type=F32)
        pre = pre_buf[k]
        inner = gelu_coeff * (pre + gelu_cubic * pre * pre * pre)
        tangent = jnp.tanh(inner)
        slope = 0.5 * (1.0 + tangent) + 0.5 * pre * (1.0 - tangent * tangent) * gelu_coeff * (
            1.0 + 3.0 * gelu_cubic * pre * pre
        )
        pre_grad = (act_grad * slope).astype(BF)
        for n in range(GROUPS):
            pg_stage[n, k] = pre_grad[:, n * PIECE : (n + 1) * PIECE]
        dots = jnp.sum(pre_grad.astype(F32) * pre, axis=-1, keepdims=True)
        extra = jnp.broadcast_to(dots, (SLOT_ROWS, 128)).astype(BF)
        scatter(
            k, pre_grad, w_in, extra, merge_send_b, merge_own_b, merge_recv_b,
            rs_send_b, rs_recv_b, merge_sem_b, 1,
        )
        return carry

    lax.fori_loop(0, CHUNKS, back, 0)

    def grads_copy(d, stage, gathered, which):
        there = lax.rem(g + d, GROUPS)
        return pltpu.make_async_remote_copy(
            stage.at[there], gathered.at[g], grads_send_sem.at[which, d], grads_sem.at[which, d],
            **to(t, part * GROUPS + there),
        )

    for d in range(1, GROUPS):
        grads_copy(d, pg_stage, pg_all, 0).start()
        grads_copy(d, act_stage, act_all, 1).start()
    pg_all[g] = pg_stage[g]
    act_all[g] = act_stage[g]

    flat = x_buf[own_k, own_i].astype(F32)
    inv = norm_scale(flat)
    held = x_buf[own_k, own_i, :, own_cols].astype(F32)
    above = u_buf[own_k, own_i, :, own_cols].astype(F32)
    gain_own = choose(
        table[GROUP_OF + own_i], [gains[n : n + 1, own_cols] for n in range(GROUPS)]
    )
    pltpu.make_async_copy(rs_recv_b, rs_recv_b, rs_sem.at[1]).wait()
    summed = total(rs_recv_b)
    pulled = summed[:, 0:QUART] * gain_own
    row_dot = summed[:, QUART : QUART + 1] * (1.0 / D)
    own_b[...] = (above + inv * pulled - held * (inv * inv * row_dot)).astype(BF)

    def final_copy(n):
        target = own_k * ROWS + n
        return target, pltpu.make_async_remote_copy(
            own_b, final_recv.at[own_j], final_send_sem.at[0], final_sem.at[0], **to(own_i, target)
        )

    @pl.when(t > 0)
    def _():
        spread(own_b, u_buf, t - 1, u_sem, 1)

    @pl.when(t == 0)
    def _():
        def one(n, carry):
            target, copy = final_copy(n)
            here = (target == r) & (own_i == 0)

            @pl.when(jnp.logical_not(here))
            def _():
                copy.start()

            @pl.when(here)
            def _():
                pltpu.make_async_copy(own_b, final_recv.at[own_j], final_sem.at[0]).start()

            return carry

        lax.fori_loop(0, ROWS, one, 0)

    def gather_rows(k, carry):
        for i in range(MICRO):
            rows = x_buf[k, i].astype(F32)
            gain = gain_row(table[GROUP_OF + i])
            normed_out[k, i] = (rows * norm_scale(rows) * gain).astype(BF)
            live = live_rows(k, table[LENGTH + i]).astype(F32)
            masked_out[k, i] = (u_buf[k, i].astype(F32) * live).astype(BF)
        return carry

    lax.fori_loop(0, CHUNKS, gather_rows, 0)

    for d in range(1, GROUPS):
        grads_copy(d, pg_stage, pg_all, 0).wait()
        grads_copy(d, act_stage, act_all, 1).wait()

    def gather_hidden(k, carry):
        for gathered, out in ((pg_all, pre_out), (act_all, act_out)):
            pieces = [
                gathered[n, k, c * ROWS : (c + 1) * ROWS, :] for n in range(GROUPS) for c in range(CAP)
            ]
            for i in range(MICRO):
                out[k, i] = choose(table[PLACE_OF + i], pieces)
        return carry

    lax.fori_loop(0, CHUNKS, gather_hidden, 0)

    @pl.when(t < last)
    def _():
        scatter_done(rs_send_f, rs_recv_f, 0)
        spread_done(own_f, x_buf, t + 1, x_sem, 0)

    scatter_done(rs_send_b, rs_recv_b, 1)

    @pl.when(t > 0)
    def _():
        spread_done(own_b, u_buf, t - 1, u_sem, 1)

    pltpu.make_async_copy(final_recv, final_recv, final_sem.at[0]).wait()
    mine = lax.broadcasted_iota(jnp.int32, (ROWS, 1), 0) == lax.rem(r, ROWS)
    for j in range(4):
        rows = jnp.where(mine, final_recv[j].astype(F32), 0.0)
        grad_out[:, j * QUART : (j + 1) * QUART] = jnp.sum(rows, axis=0, keepdims=True).astype(BF)

    @pl.when(t == 0)
    def _():
        def one(n, carry):
            target, copy = final_copy(n)

            @pl.when(jnp.logical_not((target == r) & (own_i == 0)))
            def _():
                copy.wait_send()

            return carry

        lax.fori_loop(0, ROWS, one, 0)


def small_table(wiring, lengths):
    t = lax.axis_index("section")
    g = lax.axis_index("replica") % GROUPS
    routes = lax.dynamic_index_in_dim(wiring[:, :, 0], t, 0, keepdims=False)
    order = jnp.arange(MICRO, dtype=jnp.int32)
    earlier = (routes[:, None] == routes[None, :]) & (order[None, :] < order[:, None])
    slot = jnp.sum(earlier.astype(jnp.int32), axis=1)
    here = (routes[None, :] == g) & (slot[None, :] == jnp.arange(CAP)[:, None])
    slot_mb = jnp.sum(jnp.where(here, order[None, :], 0), axis=1)
    slot_len = jnp.sum(jnp.where(here, lengths[None, :], 0), axis=1)
    merge = jnp.where(routes == g, slot, jnp.where(routes == (g ^ 1), CAP + slot, 2 * CAP))
    return jnp.concatenate([slot_mb, slot_len, merge, routes, routes * CAP + slot, lengths]).astype(jnp.int32)


def body(tokens, cotangent, wiring, lengths, in_proj, out_proj, section_gain):
    table = small_table(wiring, lengths)
    both = lax.all_gather(jnp.stack([tokens, cotangent]), "replica", axis=2, tiled=True)
    both = both.reshape(2, MICRO, CHUNKS, ROWS, D).transpose(0, 2, 1, 3, 4)
    vmem = pl.BlockSpec(memory_space=pltpu.VMEM)
    hbm = pl.BlockSpec(memory_space=pl.ANY)
    dma = pltpu.SemaphoreType.DMA
    normed, masked, pre_grad, act, grad = pl.pallas_call(
        kernel,
        name="relay",
        out_shape=(
            jax.ShapeDtypeStruct((CHUNKS, MICRO, ROWS, D), BF),
            jax.ShapeDtypeStruct((CHUNKS, MICRO, ROWS, D), BF),
            jax.ShapeDtypeStruct((CHUNKS, MICRO, ROWS, PIECE), BF),
            jax.ShapeDtypeStruct((CHUNKS, MICRO, ROWS, PIECE), BF),
            jax.ShapeDtypeStruct((1, D), BF),
        ),
        in_specs=[pl.BlockSpec(memory_space=pltpu.SMEM), hbm, hbm, hbm, hbm, vmem],
        out_specs=(vmem,) * 5,
        scratch_shapes=[
            pltpu.VMEM((CHUNKS, MICRO, ROWS, D), BF),
            pltpu.VMEM((CHUNKS, MICRO, ROWS, D), BF),
            pltpu.VMEM((D, FF_DEV), BF),
            pltpu.VMEM((D, FF_DEV), BF),
            pltpu.VMEM((GROUPS, D), F32),
            pltpu.VMEM((CHUNKS, SLOT_ROWS, FF_DEV), F32),
            pltpu.VMEM((GROUPS, CHUNKS, SLOT_ROWS, PIECE), BF),
            pltpu.VMEM((GROUPS, CHUNKS, SLOT_ROWS, PIECE), BF),
            pltpu.VMEM((GROUPS, CHUNKS, SLOT_ROWS, PIECE), BF),
            pltpu.VMEM((GROUPS, CHUNKS, SLOT_ROWS, PIECE), BF),
            pltpu.VMEM((CHUNKS, SLOT_ROWS, HALF), BF),
            pltpu.VMEM((SLOT_ROWS, HALF), BF),
            pltpu.VMEM((CHUNKS, SLOT_ROWS, HALF), BF),
            pltpu.VMEM((CHUNKS, MICRO, 2, ROWS, QUART), BF),
            pltpu.VMEM((CHIPS, ROWS, QUART), BF),
            pltpu.VMEM((ROWS, QUART), BF),
            pltpu.VMEM((CHUNKS, SLOT_ROWS, HALF + 128), BF),
            pltpu.VMEM((SLOT_ROWS, HALF + 128), BF),
            pltpu.VMEM((CHUNKS, SLOT_ROWS, HALF + 128), BF),
            pltpu.VMEM((CHUNKS, MICRO, 2, ROWS, QUART + 128), BF),
            pltpu.VMEM((CHIPS, ROWS, QUART + 128), BF),
            pltpu.VMEM((ROWS, QUART), BF),
            pltpu.VMEM((4, ROWS, QUART), BF),
            dma((4,)),
            dma((CHUNKS,)),
            dma((CHUNKS,)),
            dma((CHUNKS,)),
            dma((CHUNKS,)),
            dma((1,)),
            dma((CHUNKS,)),
            dma((CHUNKS,)),
            dma((1,)),
            dma((2,)),
            dma((2,)),
            dma((2,)),
            dma((2, GROUPS)),
            dma((2, GROUPS)),
            dma((1,)),
            dma((1,)),
            dma((1,)),
        ],
        compiler_params=pltpu.CompilerParams(
            has_side_effects=True, vmem_limit_bytes=48 * 1024 * 1024
        ),
    )(table, both[0], both[1], in_proj[0, 0], out_proj[0, 0], section_gain[0])
    rows = CHUNKS * MICRO * ROWS
    contract = (((0,), (0,)), ((), ()))
    in_grad = lax.dot_general(
        normed.reshape(rows, D), pre_grad.reshape(rows, PIECE), contract, preferred_element_type=F32
    )
    out_grad = lax.dot_general(
        masked.reshape(rows, D), act.reshape(rows, PIECE), contract, preferred_element_type=F32
    )
    return grad[None], in_grad.astype(BF)[None], out_grad.astype(BF)[None]


def solution(mesh):
    in_specs = (
        P(None, "replica", None),
        P(None, "replica", None),
        P(),
        P(),
        P("section", "replica", None, None),
        P("section", "replica", None, None),
        P("section", None, None),
    )
    out_specs = (
        P("section", "replica", None),
        P("section", None, "replica"),
        P("section", None, "replica"),
    )
    return jax.shard_map(body, mesh=mesh, in_specs=in_specs, out_specs=out_specs, check_vma=False)
```

```python
import jax
import jax.numpy as jnp
from jax import lax
from jax.experimental import pallas as pl
from jax.experimental.pallas import tpu as pltpu
from jax.sharding import PartitionSpec as P

D = 2560
FF_DEV = 640
GROUPS = 4
CAP = 2
MICRO = 4
CHUNKS = 4
ROWS = 16
HALF = D // 2
QUART = D // 4
SLOT_ROWS = CAP * ROWS
PIECE = FF_DEV // GROUPS
CHIPS = 32
LINE = 8

gelu_coeff = 0.7978845608028654
gelu_cubic = 0.044715
epsilon = 1e-05

BF = jnp.bfloat16
F32 = jnp.float32
NT = (((1,), (1,)), ((), ()))

def choose(index, values):
    picked = values[0]
    for n in range(1, len(values)):
        picked = jnp.where(index == n, values[n], picked)
    return picked


def norm_scale(rows):
    return lax.rsqrt(jnp.mean(rows * rows, axis=-1, keepdims=True) + epsilon)


def kernel(
    wiring, lengths, tokens, cotangent, w_in_hbm, w_out_hbm, gain_hbm,
    normed_out, masked_out, pre_out, act_out, grad_out,
    x_buf, u_buf, w_in, w_out, gain_rows, gains, entry_rows, entry_send, entry_recv,
    h_buf, pre_buf, inv_buf, act_buf, back_buf, pg_stage, act_stage, pg_all, act_all,
    merge_send_f, merge_own, merge_recv_f, line_send_f, line_recv_f, rs_send_f, rs_recv_f, own_f, held_recv,
    merge_send_b, merge_recv_b, line_send_b, line_recv_b, rs_send_b, rs_recv_b, own_b, above_recv, final_own, final_recv,
    load_sem, go_sem, entry_sem, entry_send_sem, x_sem, x_core_sem, u_sem, u_core_sem, core_send_sem,
    merge_sem_f, merge_sem_b, merge_send_sem, line_sem, line_send_sem, rs_sem, rs_send_sem, ag_send_sem,
    pass_sem, pass_send_sem, grads_sem, grads_send_sem, final_sem, final_send_sem,
):
    t = lax.axis_index("section")
    r = lax.axis_index("replica")
    core = lax.rem(r, 2)
    other = 1 - core
    chip = lax.div(r, 2)
    z = lax.div(r, 8)
    y = lax.rem(chip, 4)
    g = lax.rem(r, 4)
    part = lax.div(r, 4)
    last = lax.axis_size("section") - 1
    own_k = lax.rem(z + 2 * core, 4)
    own_i = 2 * lax.div(z, 4) + lax.rem(y, 2)
    own_j = 2 * core + lax.div(y, 2)
    own_cols = pl.ds(pl.multiple_of(own_j * QUART, 128), QUART)
    own_turn = jnp.maximum(own_k - 2, 0)
    mate = r + 1 - 2 * core
    my_half = pl.ds(pl.multiple_of(core * HALF, 128), HALF)
    mate_half = pl.ds(pl.multiple_of(other * HALF, 128), HALF)
    mate_rows = pl.ds(pl.multiple_of(other * HALF, HALF), HALF)
    my_rows = pl.ds(pl.multiple_of(core * HALF, HALF), HALF)

    routes = [wiring[t, 0, i] for i in range(MICRO)]
    lens = [lengths[i] for i in range(MICRO)]
    slots = []
    for i in range(MICRO):
        taken = jnp.int32(0)
        for e in range(i):
            taken = taken + jnp.where(routes[e] == routes[i], 1, 0)
        slots.append(taken)
    slot_mb, slot_len = [], []
    for c in range(CAP):
        number, length = jnp.int32(0), jnp.int32(0)
        for i in range(MICRO):
            here = (routes[i] == g) & (slots[i] == c)
            number = jnp.where(here, i, number)
            length = jnp.where(here, lens[i], length)
        slot_mb.append(number)
        slot_len.append(length)
    mate_g = g + 1 - 2 * core
    merge_from = [
        jnp.where(routes[i] == g, slots[i], jnp.where(routes[i] == mate_g, CAP + slots[i], 2 * CAP))
        for i in range(MICRO)
    ]

    def to(section, replica):
        return dict(device_id=(section, replica), device_id_type=pl.DeviceIdType.MESH)

    def start_or_keep(target_section, target, remote, source, dest, sem):
        here = (target == r) & (target_section == t)

        @pl.when(jnp.logical_not(here))
        def _():
            remote.start()

        @pl.when(here)
        def _():
            pltpu.make_async_copy(source, dest, sem).start()

    def wait_sent(target_section, target, remote):
        @pl.when(jnp.logical_not((target == r) & (target_section == t)))
        def _():
            remote.wait_send()

    def owner_z(k, oc):
        return lax.rem(k + 2 * oc, 4)

    entry_z = [owner_z(lax.div(r, ROWS), oc) for oc in range(2)]

    def entry_copy(n):
        i, j = n // 4, n % 4
        oy = 2 * (j % 2) + i % 2
        target = (entry_z[j // 2] + 4 * (i // 2)) * 8 + oy * 2 + j // 2
        source, dest = entry_send.at[i, j], entry_recv.at[lax.rem(r, ROWS)]
        return target, source, dest, pltpu.make_async_remote_copy(
            source, dest, entry_send_sem.at[0], entry_sem.at[0], **to(t, target)
        )

    in_load = pltpu.make_async_copy(w_in_hbm, w_in, load_sem.at[0])
    out_load = pltpu.make_async_copy(w_out_hbm, w_out, load_sem.at[1])
    gain_load = pltpu.make_async_copy(gain_hbm, gain_rows, load_sem.at[2])
    ends = (t == 0) | (t == last)

    @pl.when(t == 0)
    def _():
        pltpu.make_async_copy(tokens, entry_rows, load_sem.at[3]).start()

    @pl.when(t == last)
    def _():
        pltpu.make_async_copy(cotangent, entry_rows, load_sem.at[3]).start()

    gain_load.start()
    in_load.start()
    out_load.start()

    barrier = pltpu.get_barrier_semaphore()
    planes = lax.axis_size("section")
    replicas = lax.axis_size("replica")

    def tell_line(n, carry):
        for shift in (1, planes - 1):
            there = lax.rem(t + shift, planes)
            pl.semaphore_signal(barrier, inc=1, **to(there, n * 8 + y * 2 + other))
        return carry

    def tell_plane(n, carry):
        pl.semaphore_signal(barrier, inc=1, **to(t, lax.rem(r + n, replicas)))
        return carry

    lax.fori_loop(1, replicas, tell_plane, 0)
    lax.fori_loop(0, LINE, tell_line, 0)
    for shift in (1, planes - 1):
        pl.semaphore_signal(barrier, inc=1, **to(lax.rem(t + shift, planes), r))

    @pl.when(t > 0)
    def _():
        final_z = [owner_z(lax.div(r, ROWS), oc) for oc in range(2)]
        for j in range(4):
            oy = 2 * (j % 2) + lax.rem(t, 2)
            target = (final_z[j // 2] + 4 * lax.div(t, 2)) * 8 + oy * 2 + j // 2
            pl.semaphore_signal(barrier, inc=1, **to(0, target))

    @pl.when(ends)
    def _():
        pltpu.make_async_copy(tokens, entry_rows, load_sem.at[3]).wait()
        for i in range(MICRO):
            row = entry_rows[i : i + 1, :].astype(F32)
            for j in range(4):
                entry_send[i, j] = row[:, j * QUART : (j + 1) * QUART]

    gain_load.wait()
    gains[...] = gain_rows[...].astype(F32)
    pl.semaphore_wait(barrier, replicas - 1 + 2 * LINE + 2 + jnp.where((t == 0) & (own_i > 0), ROWS, 0))

    @pl.when(ends)
    def _():
        for n in range(MICRO * 4):
            target, source, dest, copy = entry_copy(n)
            start_or_keep(t, target, copy, source, dest, entry_sem.at[0])

    def entered():
        pltpu.make_async_copy(entry_recv, entry_recv, entry_sem.at[0]).wait()
        return entry_recv[...].reshape(ROWS, QUART).astype(BF)

    def gain_row(group):
        return choose(group, [gains[n : n + 1, :] for n in range(GROUPS)])

    def arrive(buf, k, sem, core_sem):
        view = buf.at[k, :, :, mate_half]
        pltpu.make_async_copy(view, view, sem.at[k]).wait()
        copy = pltpu.make_async_remote_copy(view, view, core_send_sem.at[0], core_sem.at[k], **to(t, mate))
        copy.start()
        return copy

    def slot_rows(buf, k, cols):
        rows = [buf[k, i, :, cols] for i in range(MICRO)]
        return jnp.concatenate([choose(slot_mb[c], rows) for c in range(CAP)], axis=0)

    def gain_part(cols):
        return choose(g, [gains[n : n + 1, cols] for n in range(GROUPS)])

    def slot_live(k):
        return jnp.concatenate([live_rows(k, slot_len[c]).astype(F32) for c in range(CAP)], axis=0)

    def x_stage(k):
        copy = arrive(x_buf, k, x_sem, x_core_sem)

        def half(cols, rows):
            held = slot_rows(x_buf, k, cols)
            h_buf[k, :, cols] = held
            flat = held.astype(F32)
            scaled = (flat * gain_part(cols)).astype(BF)
            squares = jnp.sum(flat * flat, axis=-1, keepdims=True)
            return squares, jnp.dot(scaled, w_in[rows, :], preferred_element_type=F32)

        mine = half(mate_half, mate_rows)
        copy.wait()
        theirs = half(my_half, my_rows)
        inv = lax.rsqrt((mine[0] + theirs[0]) * (1.0 / D) + epsilon)
        inv_buf[k] = jnp.broadcast_to(inv, (SLOT_ROWS, 128))
        pre = (mine[1] + theirs[1]) * inv
        pre_buf[k] = pre
        act = jax.nn.gelu(pre, approximate=True).astype(BF)
        act_buf[k] = act
        return act

    def u_stage(k):
        copy = arrive(u_buf, k, u_sem, u_core_sem)
        live = slot_live(k)

        def half(cols, rows):
            masked = (slot_rows(u_buf, k, cols).astype(F32) * live).astype(BF)
            return jnp.dot(masked, w_out[rows, :], preferred_element_type=F32)

        mine = half(mate_half, mate_rows)
        copy.wait()
        back_buf[k] = mine + half(my_half, my_rows)

    def merge_copy(k, send, recv, sem):
        return pltpu.make_async_remote_copy(
            send.at[k], recv.at[k], merge_send_sem.at[0], sem.at[k], **to(t, mate)
        )

    line_base = z * 8 + other

    def scatter(k, half, send, recv, line_send, line_recv, sem, way):
        send[k] = half(mate_rows, mate_half)
        copy = merge_copy(k, send, recv, sem)
        copy.start()
        merge_own[...] = half(my_rows, my_half)
        copy.wait()
        for i in range(MICRO):
            merged = choose(
                merge_from[i],
                [
                    merge_own[0:ROWS, :], merge_own[ROWS:SLOT_ROWS, :],
                    recv[k, 0:ROWS, :], recv[k, ROWS:SLOT_ROWS, :], jnp.zeros((ROWS, HALF), BF),
                ],
            )
            for jj in range(2):
                line_send[k, 2 * jj + i % 2, i // 2] = merged[:, jj * QUART : (jj + 1) * QUART]
        for there in range(4):
            pltpu.make_async_remote_copy(
                line_send.at[k, there], line_recv.at[k, y], line_send_sem.at[way], line_sem.at[way, k],
                **to(t, line_base + 2 * there),
            ).start()

    def relay(k, section, line_recv, rs_send, rs_recv, way, slot):
        pltpu.make_async_copy(line_recv.at[k], line_recv.at[k], line_sem.at[way, k]).wait()
        base = owner_z(k, other) * 8 + y * 2 + other
        for n in range(2):
            pieces = [line_recv[k, e, n].astype(F32) for e in range(4)]
            rs_send[k, n] = ((pieces[0] + pieces[1]) + (pieces[2] + pieces[3])).astype(BF)
            pltpu.make_async_remote_copy(
                rs_send.at[k, n], rs_recv.at[z], rs_send_sem.at[way], rs_sem.at[slot],
                **to(section, base + 32 * n),
            ).start()

    def relay_turn(k, section, line_recv, rs_send, rs_recv, way, slot):
        @pl.when(k > 0)
        def _():
            relay(k - 1, section, line_recv, rs_send, rs_recv, way, slot)

        @pl.when(k == CHUNKS - 1)
        def _():
            relay(k, section, line_recv, rs_send, rs_recv, way, slot)

    def scatter_done(line_send, rs_send, way):
        pltpu.make_async_copy(line_send, line_send, line_send_sem.at[way]).wait()
        pltpu.make_async_copy(rs_send, rs_send, rs_send_sem.at[way]).wait()

    def live_rows(k, length):
        position = k * ROWS + lax.broadcasted_iota(jnp.int32, (ROWS, 1), 0)
        return position < length

    spread_z = [lax.rem(z + dz, 8) * 8 + other for dz in (4, 3, 5, 2, 6, 1, 7, 0)]
    spread_y = [lax.rem(y + dy, 4) * 2 for dy in (2, 1, 3, 0)]

    def spread(source, buf, sem, way):
        for base in spread_z:
            for add in spread_y:
                pltpu.make_async_remote_copy(
                    source, buf.at[own_k, own_i, :, own_cols], ag_send_sem.at[way], sem.at[own_k],
                    **to(t, base + add),
                ).start()

    def spread_done(source, way):
        def one(n, carry):
            pltpu.make_async_copy(source, source, ag_send_sem.at[way]).wait()
            return carry

        lax.fori_loop(0, CHIPS, one, 0)

    def pass_copy(source, dest, section, way):
        return pltpu.make_async_remote_copy(
            source, dest, pass_send_sem.at[way], pass_sem.at[way], **to(section, r)
        )

    def pass_on():
        return pass_copy(own_f, held_recv, t + 1, 0)

    def pass_above():
        return pass_copy(own_b, above_recv, t - 1, 1)

    def received(dest, way):
        pltpu.make_async_copy(dest, dest, pass_sem.at[way]).wait()

    def combined(before, pieces, slot):
        pltpu.make_async_copy(pieces, pieces, rs_sem.at[slot]).wait()
        return (before.astype(F32) + jnp.sum(pieces[...].astype(F32), axis=0)).astype(BF)

    def own_forward():
        @pl.when(t == 0)
        def _():
            own_f[...] = entered()

            @pl.when(own_k > 0)
            def _():
                pl.semaphore_wait(go_sem, 1)

        @pl.when(t > 0)
        def _():
            received(held_recv, 0)
            own_f[...] = combined(held_recv[...], rs_recv_f, 0)

        spread(own_f, x_buf, x_sem, 0)

        @pl.when((t == 0) & (own_k < CHUNKS - 1))
        def _():
            pl.semaphore_signal(go_sem, inc=1, **to(t, lax.rem(r + 8, replicas)))

        @pl.when(t < last)
        def _():
            pass_on().start()


    def own_backward():
        @pl.when(t == last)
        def _():
            own_b[...] = entered()

        @pl.when(t < last)
        def _():
            received(above_recv, 1)
            own_b[...] = combined(above_recv[...], rs_recv_b.at[0], 1)

        spread(own_b, u_buf, u_sem, 1)

        @pl.when(t > 0)
        def _():
            pass_above().start()

    def gather_normed(k, carry):
        for i in range(MICRO):
            rows = x_buf[k, i].astype(F32)
            gain = gain_row(routes[i])
            normed_out[k, i] = (rows * norm_scale(rows) * gain).astype(BF)
        return carry

    def gather_masked(k, carry):
        for i in range(MICRO):
            live = live_rows(k, lens[i]).astype(F32)
            masked_out[k, i] = (u_buf[k, i].astype(F32) * live).astype(BF)
        return carry

    def grads_copy(d, stage, gathered, which):
        there = lax.rem(g + d, GROUPS)
        return pltpu.make_async_remote_copy(
            stage.at[there], gathered.at[g], grads_send_sem.at[which, d], grads_sem.at[which, d],
            **to(t, part * GROUPS + there),
        )

    def send_act():
        for d in range(1, GROUPS):
            grads_copy(d, act_stage, act_all, 1).start()

    def split_act(k, carry):
        for n in range(GROUPS):
            act_stage[n, k] = act_buf[k, :, n * PIECE : (n + 1) * PIECE]
        return carry

    @pl.when(t == last)
    def _():
        own_backward()
        out_load.wait()

        def step(k, carry):
            u_stage(k)
            return carry

        lax.fori_loop(0, CHUNKS, step, 0)
        lax.fori_loop(0, CHUNKS, gather_masked, 0)
        in_load.wait()

    @pl.when(t < last)
    def _():
        in_load.wait()
        out_load.wait()

        def step(k, carry):
            @pl.when(k == own_turn)
            def _():
                own_forward()

            act = (x_stage(k).astype(F32) * slot_live(k)).astype(BF)

            def half(rows, cols):
                return lax.dot_general(act, w_out[rows, :], NT, preferred_element_type=F32).astype(BF)

            scatter(k, half, merge_send_f, merge_recv_f, line_send_f, line_recv_f, merge_sem_f, 0)
            relay_turn(k, t + 1, line_recv_f, rs_send_f, rs_recv_f, 0, 0)
            return carry

        lax.fori_loop(0, CHUNKS, step, 0)
        lax.fori_loop(0, CHUNKS, split_act, 0)
        send_act()
        lax.fori_loop(0, CHUNKS, gather_normed, 0)

    back_section = jnp.maximum(t - 1, 0)
    back_slot = jnp.where(t == 0, 1, 0)

    def back(k, carry):
        @pl.when((t == last) & (k == own_turn))
        def _():
            own_forward()

        @pl.when((t < last) & (k == own_turn))
        def _():
            own_backward()

        @pl.when(t == last)
        def _():
            x_stage(k)

        @pl.when(t < last)
        def _():
            u_stage(k)

        pre = pre_buf[k]
        inner = gelu_coeff * (pre + gelu_cubic * pre * pre * pre)
        tangent = jnp.tanh(inner)
        slope = 0.5 * (1.0 + tangent) + 0.5 * pre * (1.0 - tangent * tangent) * gelu_coeff * (
            1.0 + 3.0 * gelu_cubic * pre * pre
        )
        pre_grad = (back_buf[k] * slope).astype(BF)
        inv = inv_buf[k, :, 0:1]
        dots = jnp.sum(pre_grad.astype(F32) * pre, axis=-1, keepdims=True) * (inv * inv * (1.0 / D))

        def half(rows, cols):
            value = lax.dot_general(pre_grad, w_in[rows, :], NT, preferred_element_type=F32)
            return (value * inv * gain_part(cols) - h_buf[k, :, cols].astype(F32) * dots).astype(BF)

        scatter(k, half, merge_send_b, merge_recv_b, line_send_b, line_recv_b, merge_sem_b, 1)
        for n in range(GROUPS):
            pg_stage[n, k] = pre_grad[:, n * PIECE : (n + 1) * PIECE]
        relay_turn(k, back_section, line_recv_b, rs_send_b, rs_recv_b.at[back_slot], 1, 1 + back_slot)
        return carry

    lax.fori_loop(0, CHUNKS, back, 0)

    for d in range(1, GROUPS):
        grads_copy(d, pg_stage, pg_all, 0).start()

    @pl.when(t == last)
    def _():
        lax.fori_loop(0, CHUNKS, split_act, 0)
        send_act()
        lax.fori_loop(0, CHUNKS, gather_normed, 0)

    @pl.when(t < last)
    def _():
        lax.fori_loop(0, CHUNKS, gather_masked, 0)

    pg_all[g] = pg_stage[g]
    act_all[g] = act_stage[g]

    def final_copy(n):
        target = own_k * ROWS + n
        return target, pltpu.make_async_remote_copy(
            final_own, final_recv.at[own_j], final_send_sem.at[0], final_sem.at[0], **to(own_i, target)
        )

    @pl.when(t == 0)
    def _():
        final_own[...] = combined(own_b[...], rs_recv_b.at[1], 2)

        def one(n, carry):
            target, copy = final_copy(n)
            start_or_keep(own_i, target, copy, final_own, final_recv.at[own_j], final_sem.at[0])
            return carry

        lax.fori_loop(0, ROWS, one, 0)

    for d in range(1, GROUPS):
        grads_copy(d, pg_stage, pg_all, 0).wait()
        grads_copy(d, act_stage, act_all, 1).wait()

    def gather_hidden(k, carry):
        for gathered, out in ((pg_all, pre_out), (act_all, act_out)):
            pieces = [
                gathered[n, k, c * ROWS : (c + 1) * ROWS, :] for n in range(GROUPS) for c in range(CAP)
            ]
            for i in range(MICRO):
                out[k, i] = choose(routes[i] * CAP + slots[i], pieces)
        return carry

    lax.fori_loop(0, CHUNKS, gather_hidden, 0)

    @pl.when((t == 0) | (t == last))
    def _():
        for n in range(MICRO * 4):
            target, source, dest, copy = entry_copy(n)
            wait_sent(t, target, copy)

    spread_done(own_f, 0)
    spread_done(own_b, 1)

    @pl.when(t < last)
    def _():
        scatter_done(line_send_f, rs_send_f, 0)
        pass_on().wait_send()

    scatter_done(line_send_b, rs_send_b, 1)

    @pl.when(t > 0)
    def _():
        pass_above().wait_send()

    pltpu.make_async_copy(final_recv, final_recv, final_sem.at[0]).wait()
    mine = lax.broadcasted_iota(jnp.int32, (ROWS, 1), 0) == lax.rem(r, ROWS)
    for j in range(4):
        rows = jnp.where(mine, final_recv[j].astype(F32), 0.0)
        grad_out[:, j * QUART : (j + 1) * QUART] = jnp.sum(rows, axis=0, keepdims=True).astype(BF)

    @pl.when(t == 0)
    def _():
        def one(n, carry):
            target, copy = final_copy(n)
            wait_sent(own_i, target, copy)
            return carry

        lax.fori_loop(0, ROWS, one, 0)


def body(tokens, cotangent, wiring, lengths, in_proj, out_proj, section_gain):
    vmem = pl.BlockSpec(memory_space=pltpu.VMEM)
    smem = pl.BlockSpec(memory_space=pltpu.SMEM)
    hbm = pl.BlockSpec(memory_space=pl.ANY)
    dma = pltpu.SemaphoreType.DMA
    normed, masked, pre_grad, act, grad = pl.pallas_call(
        kernel,
        name="relay",
        out_shape=(
            jax.ShapeDtypeStruct((CHUNKS, MICRO, ROWS, D), BF),
            jax.ShapeDtypeStruct((CHUNKS, MICRO, ROWS, D), BF),
            jax.ShapeDtypeStruct((CHUNKS, MICRO, ROWS, PIECE), BF),
            jax.ShapeDtypeStruct((CHUNKS, MICRO, ROWS, PIECE), BF),
            jax.ShapeDtypeStruct((1, D), BF),
        ),
        in_specs=[smem, smem, hbm, hbm, hbm, hbm, hbm],
        out_specs=(vmem,) * 5,
        scratch_shapes=[
            pltpu.VMEM((CHUNKS, MICRO, ROWS, D), BF),
            pltpu.VMEM((CHUNKS, MICRO, ROWS, D), BF),
            pltpu.VMEM((D, FF_DEV), BF),
            pltpu.VMEM((D, FF_DEV), BF),
            pltpu.VMEM((GROUPS, D), BF),
            pltpu.VMEM((GROUPS, D), F32),
            pltpu.VMEM((MICRO, D), BF),
            pltpu.VMEM((MICRO, 4, 1, QUART), F32),
            pltpu.VMEM((ROWS, 1, QUART), F32),
            pltpu.VMEM((CHUNKS, SLOT_ROWS, D), BF),
            pltpu.VMEM((CHUNKS, SLOT_ROWS, FF_DEV), F32),
            pltpu.VMEM((CHUNKS, SLOT_ROWS, 128), F32),
            pltpu.VMEM((CHUNKS, SLOT_ROWS, FF_DEV), BF),
            pltpu.VMEM((CHUNKS, SLOT_ROWS, FF_DEV), F32),
            pltpu.VMEM((GROUPS, CHUNKS, SLOT_ROWS, PIECE), BF),
            pltpu.VMEM((GROUPS, CHUNKS, SLOT_ROWS, PIECE), BF),
            pltpu.VMEM((GROUPS, CHUNKS, SLOT_ROWS, PIECE), BF),
            pltpu.VMEM((GROUPS, CHUNKS, SLOT_ROWS, PIECE), BF),
            pltpu.VMEM((CHUNKS, SLOT_ROWS, HALF), BF),
            pltpu.VMEM((SLOT_ROWS, HALF), BF),
            pltpu.VMEM((CHUNKS, SLOT_ROWS, HALF), BF),
            pltpu.VMEM((CHUNKS, 4, 2, ROWS, QUART), BF),
            pltpu.VMEM((CHUNKS, 4, 2, ROWS, QUART), BF),
            pltpu.VMEM((CHUNKS, 2, ROWS, QUART), BF),
            pltpu.VMEM((LINE, ROWS, QUART), BF),
            pltpu.VMEM((ROWS, QUART), BF),
            pltpu.VMEM((ROWS, QUART), BF),
            pltpu.VMEM((CHUNKS, SLOT_ROWS, HALF), BF),
            pltpu.VMEM((CHUNKS, SLOT_ROWS, HALF), BF),
            pltpu.VMEM((CHUNKS, 4, 2, ROWS, QUART), BF),
            pltpu.VMEM((CHUNKS, 4, 2, ROWS, QUART), BF),
            pltpu.VMEM((CHUNKS, 2, ROWS, QUART), BF),
            pltpu.VMEM((2, LINE, ROWS, QUART), BF),
            pltpu.VMEM((ROWS, QUART), BF),
            pltpu.VMEM((ROWS, QUART), BF),
            pltpu.VMEM((ROWS, QUART), BF),
            pltpu.VMEM((4, ROWS, QUART), BF),
            dma((4,)),
            pltpu.SemaphoreType.REGULAR,
            dma((1,)),
            dma((1,)),
            dma((CHUNKS,)),
            dma((CHUNKS,)),
            dma((CHUNKS,)),
            dma((CHUNKS,)),
            dma((1,)),
            dma((CHUNKS,)),
            dma((CHUNKS,)),
            dma((1,)),
            dma((2, CHUNKS)),
            dma((2,)),
            dma((3,)),
            dma((2,)),
            dma((2,)),
            dma((2,)),
            dma((2,)),
            dma((2, GROUPS)),
            dma((2, GROUPS)),
            dma((1,)),
            dma((1,)),
        ],
        compiler_params=pltpu.CompilerParams(
            collective_id=0, has_side_effects=True, vmem_limit_bytes=63 * 1024 * 1024
        ),
    )(wiring.transpose(0, 2, 1), lengths, tokens.reshape(MICRO, D), cotangent.reshape(MICRO, D), in_proj[0, 0], out_proj[0, 0], section_gain[0])
    rows = CHUNKS * MICRO * ROWS
    contract = (((0,), (0,)), ((), ()))
    in_grad = lax.dot_general(
        normed.reshape(rows, D), pre_grad.reshape(rows, PIECE), contract, preferred_element_type=F32
    )
    out_grad = lax.dot_general(
        masked.reshape(rows, D), act.reshape(rows, PIECE), contract, preferred_element_type=F32
    )
    return grad[None], in_grad.astype(BF)[None], out_grad.astype(BF)[None]


def solution(mesh):
    in_specs = (
        P(None, "replica", None),
        P(None, "replica", None),
        P(),
        P(),
        P("section", "replica", None, None),
        P("section", "replica", None, None),
        P("section", None, None),
    )
    out_specs = (
        P("section", "replica", None),
        P("section", None, "replica"),
        P("section", None, "replica"),
    )
    return jax.shard_map(body, mesh=mesh, in_specs=in_specs, out_specs=out_specs, check_vma=False)
```

```python
import jax
import jax.numpy as jnp
from jax import lax
from jax.experimental import pallas as pl
from jax.experimental.pallas import tpu as pltpu
from jax.sharding import PartitionSpec as P

D = 2560
FF_DEV = 640
GROUPS = 4
CAP = 2
MICRO = 4
CHUNKS = 4
ROWS = 16
HALF = D // 2
QUART = D // 4
SLOT_ROWS = CAP * ROWS
PIECE = FF_DEV // GROUPS
CHIPS = 32
LINE = 8
SPREAD_ORDER = sorted(
    ((dz, dy) for dz in range(8) for dy in range(4)),
    key=lambda shift: -(min(shift[0], 8 - shift[0]) + min(shift[1], 4 - shift[1])),
)

gelu_coeff = 0.7978845608028654
gelu_cubic = 0.044715
epsilon = 1e-05

BF = jnp.bfloat16
F32 = jnp.float32
NT = (((1,), (1,)), ((), ()))

def choose(index, values):
    picked = values[0]
    for n in range(1, len(values)):
        picked = jnp.where(index == n, values[n], picked)
    return picked


def norm_scale(rows):
    return lax.rsqrt(jnp.mean(rows * rows, axis=-1, keepdims=True) + epsilon)


def kernel(
    wiring, lengths, tokens, cotangent, w_in_hbm, w_out_hbm, gain_hbm,
    normed_out, masked_out, pre_out, act_out, grad_out,
    x_buf, u_buf, w_in, w_out, gain_rows, gains, entry_rows, entry_send, entry_recv,
    h_buf, pre_buf, inv_buf, act_buf, back_buf, pg_stage, act_stage, pg_all, act_all,
    merge_send_f, merge_own, merge_recv_f, line_send_f, line_recv_f, rs_send_f, rs_recv_f, own_f, held_recv,
    merge_send_b, merge_recv_b, line_send_b, line_recv_b, rs_send_b, rs_recv_b, own_b, above_recv,
    final_above, final_own, final_recv,
    load_sem, go_sem, entry_sem, entry_send_sem, x_sem, x_core_sem, u_sem, u_core_sem, core_send_sem,
    merge_sem_f, merge_sem_b, merge_send_sem, line_sem, line_send_sem, rs_sem, rs_send_sem, ag_send_sem,
    pass_sem, pass_send_sem, above_sem, above_send_sem, grads_sem, grads_send_sem, final_sem, final_send_sem,
):
    t = lax.axis_index("section")
    r = lax.axis_index("replica")
    core = lax.rem(r, 2)
    other = 1 - core
    chip = lax.div(r, 2)
    z = lax.div(r, 8)
    y = lax.rem(chip, 4)
    g = lax.rem(r, 4)
    part = lax.div(r, 4)
    last = lax.axis_size("section") - 1
    own_k = lax.rem(z + 2 * core, 4)
    own_i = 2 * lax.div(z, 4) + lax.rem(y, 2)
    own_j = 2 * core + lax.div(y, 2)
    own_cols = pl.ds(pl.multiple_of(own_j * QUART, 128), QUART)
    own_turn = jnp.maximum(own_k - 2, 0)
    mate = r + 1 - 2 * core
    my_half = pl.ds(pl.multiple_of(core * HALF, 128), HALF)
    mate_half = pl.ds(pl.multiple_of(other * HALF, 128), HALF)
    mate_rows = pl.ds(pl.multiple_of(other * HALF, HALF), HALF)
    my_rows = pl.ds(pl.multiple_of(core * HALF, HALF), HALF)

    routes = [wiring[t, 0, i] for i in range(MICRO)]
    lens = [lengths[i] for i in range(MICRO)]
    slots = []
    for i in range(MICRO):
        taken = jnp.int32(0)
        for e in range(i):
            taken = taken + jnp.where(routes[e] == routes[i], 1, 0)
        slots.append(taken)
    slot_mb, slot_len = [], []
    for c in range(CAP):
        number, length = jnp.int32(0), jnp.int32(0)
        for i in range(MICRO):
            here = (routes[i] == g) & (slots[i] == c)
            number = jnp.where(here, i, number)
            length = jnp.where(here, lens[i], length)
        slot_mb.append(number)
        slot_len.append(length)
    mate_g = g + 1 - 2 * core
    merge_from = [
        jnp.where(routes[i] == g, slots[i], jnp.where(routes[i] == mate_g, CAP + slots[i], 2 * CAP))
        for i in range(MICRO)
    ]

    def to(section, replica):
        return dict(device_id=(section, replica), device_id_type=pl.DeviceIdType.MESH)

    def start_or_keep(target_section, target, remote, source, dest, sem):
        here = (target == r) & (target_section == t)

        @pl.when(jnp.logical_not(here))
        def _():
            remote.start()

        @pl.when(here)
        def _():
            pltpu.make_async_copy(source, dest, sem).start()

    def wait_sent(target_section, target, remote):
        @pl.when(jnp.logical_not((target == r) & (target_section == t)))
        def _():
            remote.wait_send()

    def owner_z(k, oc):
        return lax.rem(k + 2 * oc, 4)

    entry_z = [owner_z(lax.div(r, ROWS), oc) for oc in range(2)]

    def entry_copy(n):
        i, j = n // 4, n % 4
        oy = 2 * (j % 2) + i % 2
        target = (entry_z[j // 2] + 4 * (i // 2)) * 8 + oy * 2 + j // 2
        source, dest = entry_send.at[i, j], entry_recv.at[lax.rem(r, ROWS)]
        return target, source, dest, pltpu.make_async_remote_copy(
            source, dest, entry_send_sem.at[0], entry_sem.at[0], **to(t, target)
        )

    in_load = pltpu.make_async_copy(w_in_hbm, w_in, load_sem.at[0])
    out_load = pltpu.make_async_copy(w_out_hbm, w_out, load_sem.at[1])
    gain_load = pltpu.make_async_copy(gain_hbm, gain_rows, load_sem.at[2])
    ends = (t == 0) | (t == last)

    @pl.when(t == 0)
    def _():
        pltpu.make_async_copy(tokens, entry_rows, load_sem.at[3]).start()

    @pl.when(t == last)
    def _():
        pltpu.make_async_copy(cotangent, entry_rows, load_sem.at[3]).start()

    gain_load.start()
    in_load.start()
    out_load.start()

    barrier = pltpu.get_barrier_semaphore()
    planes = lax.axis_size("section")
    replicas = lax.axis_size("replica")

    def tell_line(n, carry):
        for shift in (1, planes - 1):
            there = lax.rem(t + shift, planes)
            pl.semaphore_signal(barrier, inc=1, **to(there, n * 8 + y * 2 + other))
        return carry

    def tell_plane(n, carry):
        pl.semaphore_signal(barrier, inc=1, **to(t, lax.rem(r + n, replicas)))
        return carry

    lax.fori_loop(1, replicas, tell_plane, 0)
    lax.fori_loop(0, LINE, tell_line, 0)
    for shift in (1, planes - 1):
        pl.semaphore_signal(barrier, inc=1, **to(lax.rem(t + shift, planes), r))

    is_final = (lax.rem(y, 2) == lax.rem(t, 2)) & (lax.rem(z, 2) == lax.div(t, 2))
    final_k = lax.div(z, 2)
    final_j = 2 * core + lax.div(y, 2)

    @pl.when(t == 2)
    def _():
        def tell_first(n, carry):
            pl.semaphore_signal(barrier, inc=1, **to(0, n * 8 + y * 2 + other))
            return carry

        lax.fori_loop(0, LINE, tell_first, 0)

    @pl.when((t > 0) & is_final)
    def _():
        holder = (4 * lax.div(t, 2) + owner_z(final_k, core)) * 8 + y * 2 + core
        pl.semaphore_signal(barrier, inc=1, **to(0, holder))

    @pl.when(ends)
    def _():
        pltpu.make_async_copy(tokens, entry_rows, load_sem.at[3]).wait()
        for i in range(MICRO):
            row = entry_rows[i : i + 1, :].astype(F32)
            for j in range(4):
                entry_send[i, j] = row[:, j * QUART : (j + 1) * QUART]

    gain_load.wait()
    gains[...] = gain_rows[...].astype(F32)
    pl.semaphore_wait(barrier, replicas - 1 + 2 * LINE + 2 + jnp.where(t == 0, LINE + jnp.where(own_i > 0, 1, 0), 0))

    @pl.when(ends)
    def _():
        for n in range(MICRO * 4):
            target, source, dest, copy = entry_copy(n)
            start_or_keep(t, target, copy, source, dest, entry_sem.at[0])

    def entered():
        pltpu.make_async_copy(entry_recv, entry_recv, entry_sem.at[0]).wait()
        return entry_recv[...].reshape(ROWS, QUART).astype(BF)

    def gain_row(group):
        return choose(group, [gains[n : n + 1, :] for n in range(GROUPS)])

    def arrive(buf, k, sem, core_sem):
        view = buf.at[k, :, :, mate_half]
        pltpu.make_async_copy(view, view, sem.at[k]).wait()
        copy = pltpu.make_async_remote_copy(view, view, core_send_sem.at[0], core_sem.at[k], **to(t, mate))
        copy.start()
        return copy

    def slot_rows(buf, k, cols):
        rows = [buf[k, i, :, cols] for i in range(MICRO)]
        return jnp.concatenate([choose(slot_mb[c], rows) for c in range(CAP)], axis=0)

    def gain_part(cols):
        return choose(g, [gains[n : n + 1, cols] for n in range(GROUPS)])

    def slot_live(k):
        return jnp.concatenate([live_rows(k, slot_len[c]).astype(F32) for c in range(CAP)], axis=0)

    def x_stage(k):
        copy = arrive(x_buf, k, x_sem, x_core_sem)

        def half(cols, rows):
            held = slot_rows(x_buf, k, cols)
            h_buf[k, :, cols] = held
            flat = held.astype(F32)
            scaled = (flat * gain_part(cols)).astype(BF)
            squares = jnp.sum(flat * flat, axis=-1, keepdims=True)
            return squares, jnp.dot(scaled, w_in[rows, :], preferred_element_type=F32)

        mine = half(mate_half, mate_rows)
        copy.wait()
        theirs = half(my_half, my_rows)
        inv = lax.rsqrt((mine[0] + theirs[0]) * (1.0 / D) + epsilon)
        inv_buf[k] = jnp.broadcast_to(inv, (SLOT_ROWS, 128))
        pre = (mine[1] + theirs[1]) * inv
        pre_buf[k] = pre
        act = jax.nn.gelu(pre, approximate=True).astype(BF)
        act_buf[k] = act
        return act

    def u_stage(k):
        copy = arrive(u_buf, k, u_sem, u_core_sem)
        live = slot_live(k)

        def half(cols, rows):
            masked = (slot_rows(u_buf, k, cols).astype(F32) * live).astype(BF)
            return jnp.dot(masked, w_out[rows, :], preferred_element_type=F32)

        mine = half(mate_half, mate_rows)
        copy.wait()
        back_buf[k] = mine + half(my_half, my_rows)

    def merge_copy(k, send, recv, sem):
        return pltpu.make_async_remote_copy(
            send.at[k], recv.at[k], merge_send_sem.at[0], sem.at[k], **to(t, mate)
        )

    line_base = z * 8 + other

    def scatter(k, half, send, recv, line_send, line_recv, sem, way):
        send[k] = half(mate_rows, mate_half)
        copy = merge_copy(k, send, recv, sem)
        copy.start()
        merge_own[...] = half(my_rows, my_half)
        copy.wait()
        for i in range(MICRO):
            merged = choose(
                merge_from[i],
                [
                    merge_own[0:ROWS, :], merge_own[ROWS:SLOT_ROWS, :],
                    recv[k, 0:ROWS, :], recv[k, ROWS:SLOT_ROWS, :], jnp.zeros((ROWS, HALF), BF),
                ],
            )
            for jj in range(2):
                line_send[k, 2 * jj + i % 2, i // 2] = merged[:, jj * QUART : (jj + 1) * QUART]
        for dy in (2, 1, 3, 0):
            there = lax.rem(y + dy, 4)
            pltpu.make_async_remote_copy(
                line_send.at[k, there], line_recv.at[k, y], line_send_sem.at[way], line_sem.at[way, k],
                **to(t, line_base + 2 * there),
            ).start()

    def relay(k, target, line_recv, rs_send, rs_recv, way, slot):
        pltpu.make_async_copy(line_recv.at[k], line_recv.at[k], line_sem.at[way, k]).wait()
        for n in range(2):
            section, there = target(k, n)
            pieces = [line_recv[k, e, n].astype(F32) for e in range(4)]
            rs_send[k, n] = ((pieces[0] + pieces[1]) + (pieces[2] + pieces[3])).astype(BF)
            pltpu.make_async_remote_copy(
                rs_send.at[k, n], rs_recv.at[z], rs_send_sem.at[way], rs_sem.at[slot],
                **to(section, there),
            ).start()

    def forward_target(k, n):
        return t + 1, (owner_z(k, other) + 4 * n) * 8 + y * 2 + other

    def backward_target(k, n):
        section = jnp.where(t == 0, 2 * n + lax.rem(y, 2), t - 1)
        line = jnp.where(t == 0, 2 * k + n, owner_z(k, other) + 4 * n)
        return section, line * 8 + y * 2 + other

    def relay_turn(k, target, line_recv, rs_send, rs_recv, way, slot):
        @pl.when(k > 0)
        def _():
            relay(k - 1, target, line_recv, rs_send, rs_recv, way, slot)

        @pl.when(k == CHUNKS - 1)
        def _():
            relay(k, target, line_recv, rs_send, rs_recv, way, slot)

    def scatter_done(line_send, rs_send, way):
        pltpu.make_async_copy(line_send, line_send, line_send_sem.at[way]).wait()
        pltpu.make_async_copy(rs_send, rs_send, rs_send_sem.at[way]).wait()

    def live_rows(k, length):
        position = k * ROWS + lax.broadcasted_iota(jnp.int32, (ROWS, 1), 0)
        return position < length

    spread_z = [lax.rem(z + dz, 8) * 8 + other for dz in range(8)]
    spread_y = [lax.rem(y + dy, 4) * 2 for dy in range(4)]

    def spread(source, buf, sem, way):
        for dz, dy in SPREAD_ORDER:
            pltpu.make_async_remote_copy(
                source, buf.at[own_k, own_i, :, own_cols], ag_send_sem.at[way], sem.at[own_k],
                **to(t, spread_z[dz] + spread_y[dy]),
            ).start()

    def spread_done(source, way):
        def one(n, carry):
            pltpu.make_async_copy(source, source, ag_send_sem.at[way]).wait()
            return carry

        lax.fori_loop(0, CHIPS, one, 0)

    def pass_copy(source, dest, section, way):
        return pltpu.make_async_remote_copy(
            source, dest, pass_send_sem.at[way], pass_sem.at[way], **to(section, r)
        )

    def pass_on():
        return pass_copy(own_f, held_recv, t + 1, 0)

    def final_above_copy():
        target = (2 * own_k + lax.div(own_i, 2)) * 8 + y * 2 + core
        return target, pltpu.make_async_remote_copy(
            own_b, final_above, above_send_sem.at[0], above_sem.at[0], **to(own_i, target)
        )

    def pass_above():
        return pass_copy(own_b, above_recv, t - 1, 1)

    def received(dest, way):
        pltpu.make_async_copy(dest, dest, pass_sem.at[way]).wait()

    def combined(before, pieces, slot):
        pltpu.make_async_copy(pieces, pieces, rs_sem.at[slot]).wait()
        return (before.astype(F32) + jnp.sum(pieces[...].astype(F32), axis=0)).astype(BF)

    def own_forward():
        @pl.when(t == 0)
        def _():
            own_f[...] = entered()

            @pl.when(own_k > 0)
            def _():
                pl.semaphore_wait(go_sem, 1)

        @pl.when(t > 0)
        def _():
            received(held_recv, 0)
            own_f[...] = combined(held_recv[...], rs_recv_f, 0)

        spread(own_f, x_buf, x_sem, 0)

        @pl.when((t == 0) & (own_k < CHUNKS - 1))
        def _():
            pl.semaphore_signal(go_sem, inc=1, **to(t, lax.rem(r + 8, replicas)))

        @pl.when(t < last)
        def _():
            pass_on().start()


    def own_backward():
        @pl.when(t == last)
        def _():
            own_b[...] = entered()

        @pl.when(t < last)
        def _():
            received(above_recv, 1)
            own_b[...] = combined(above_recv[...], rs_recv_b.at[0], 1)

        spread(own_b, u_buf, u_sem, 1)

        @pl.when(t > 0)
        def _():
            pass_above().start()

        @pl.when(t == 0)
        def _():
            target, copy = final_above_copy()
            start_or_keep(own_i, target, copy, own_b, final_above, above_sem.at[0])

    def gather_normed(k, carry):
        for i in range(MICRO):
            rows = x_buf[k, i].astype(F32)
            gain = gain_row(routes[i])
            normed_out[k, i] = (rows * norm_scale(rows) * gain).astype(BF)
        return carry

    def gather_masked(k, carry):
        for i in range(MICRO):
            live = live_rows(k, lens[i]).astype(F32)
            masked_out[k, i] = (u_buf[k, i].astype(F32) * live).astype(BF)
        return carry

    def grads_copy(d, stage, gathered, which):
        there = lax.rem(g + d, GROUPS)
        return pltpu.make_async_remote_copy(
            stage.at[there], gathered.at[g], grads_send_sem.at[which, d], grads_sem.at[which, d],
            **to(t, part * GROUPS + there),
        )

    def send_act():
        for d in range(1, GROUPS):
            grads_copy(d, act_stage, act_all, 1).start()

    def split_act(k, carry):
        for n in range(GROUPS):
            act_stage[n, k] = act_buf[k, :, n * PIECE : (n + 1) * PIECE]
        return carry

    @pl.when(t == last)
    def _():
        own_backward()
        out_load.wait()

        def step(k, carry):
            u_stage(k)
            return carry

        lax.fori_loop(0, CHUNKS, step, 0)
        lax.fori_loop(0, CHUNKS, gather_masked, 0)
        in_load.wait()

    @pl.when(t < last)
    def _():
        in_load.wait()
        out_load.wait()

        def step(k, carry):
            @pl.when(k == own_turn)
            def _():
                own_forward()

            act = (x_stage(k).astype(F32) * slot_live(k)).astype(BF)

            def half(rows, cols):
                return lax.dot_general(act, w_out[rows, :], NT, preferred_element_type=F32).astype(BF)

            scatter(k, half, merge_send_f, merge_recv_f, line_send_f, line_recv_f, merge_sem_f, 0)
            relay_turn(k, forward_target, line_recv_f, rs_send_f, rs_recv_f, 0, 0)
            return carry

        lax.fori_loop(0, CHUNKS, step, 0)
        lax.fori_loop(0, CHUNKS, split_act, 0)
        send_act()
        lax.fori_loop(0, CHUNKS, gather_normed, 0)

    back_slot = jnp.where(t == 0, 1, 0)

    def back(k, carry):
        @pl.when((t == last) & (k == own_turn))
        def _():
            own_forward()

        @pl.when((t < last) & (k == own_turn))
        def _():
            own_backward()

        @pl.when(t == last)
        def _():
            x_stage(k)

        @pl.when(t < last)
        def _():
            u_stage(k)

        pre = pre_buf[k]
        inner = gelu_coeff * (pre + gelu_cubic * pre * pre * pre)
        tangent = jnp.tanh(inner)
        slope = 0.5 * (1.0 + tangent) + 0.5 * pre * (1.0 - tangent * tangent) * gelu_coeff * (
            1.0 + 3.0 * gelu_cubic * pre * pre
        )
        pre_grad = (back_buf[k] * slope).astype(BF)
        inv = inv_buf[k, :, 0:1]
        dots = jnp.sum(pre_grad.astype(F32) * pre, axis=-1, keepdims=True) * (inv * inv * (1.0 / D))

        def half(rows, cols):
            value = lax.dot_general(pre_grad, w_in[rows, :], NT, preferred_element_type=F32)
            return (value * inv * gain_part(cols) - h_buf[k, :, cols].astype(F32) * dots).astype(BF)

        scatter(k, half, merge_send_b, merge_recv_b, line_send_b, line_recv_b, merge_sem_b, 1)
        for n in range(GROUPS):
            pg_stage[n, k] = pre_grad[:, n * PIECE : (n + 1) * PIECE]
        relay_turn(k, backward_target, line_recv_b, rs_send_b, rs_recv_b.at[back_slot], 1, 1 + back_slot)
        return carry

    lax.fori_loop(0, CHUNKS, back, 0)

    for d in range(1, GROUPS):
        grads_copy(d, pg_stage, pg_all, 0).start()

    @pl.when(t == last)
    def _():
        lax.fori_loop(0, CHUNKS, split_act, 0)
        send_act()
        lax.fori_loop(0, CHUNKS, gather_normed, 0)

    @pl.when(t < last)
    def _():
        lax.fori_loop(0, CHUNKS, gather_masked, 0)

    pg_all[g] = pg_stage[g]
    act_all[g] = act_stage[g]

    def final_copy(n):
        target = final_k * ROWS + n
        return target, pltpu.make_async_remote_copy(
            final_own, final_recv.at[final_j], final_send_sem.at[0], final_sem.at[0], **to(t, target)
        )

    def send_final():
        pltpu.make_async_copy(final_above, final_above, above_sem.at[0]).wait()
        final_own[...] = combined(final_above[...], rs_recv_b.at[1], 2)

        def one(n, carry):
            target, copy = final_copy(n)
            start_or_keep(t, target, copy, final_own, final_recv.at[final_j], final_sem.at[0])
            return carry

        lax.fori_loop(0, ROWS, one, 0)

    for d in range(1, GROUPS):
        grads_copy(d, pg_stage, pg_all, 0).wait()
        grads_copy(d, act_stage, act_all, 1).wait()

    def gather_hidden(k, carry):
        for gathered, out in ((pg_all, pre_out), (act_all, act_out)):
            pieces = [
                gathered[n, k, c * ROWS : (c + 1) * ROWS, :] for n in range(GROUPS) for c in range(CAP)
            ]
            for i in range(MICRO):
                out[k, i] = choose(routes[i] * CAP + slots[i], pieces)
        return carry

    @pl.when(t > 0)
    def _():
        lax.fori_loop(0, CHUNKS, gather_hidden, 0)

    @pl.when(is_final)
    def _():
        send_final()

    @pl.when(t == 0)
    def _():
        lax.fori_loop(0, CHUNKS, gather_hidden, 0)

    @pl.when((t == 0) | (t == last))
    def _():
        for n in range(MICRO * 4):
            target, source, dest, copy = entry_copy(n)
            wait_sent(t, target, copy)

    spread_done(own_f, 0)
    spread_done(own_b, 1)

    @pl.when(t < last)
    def _():
        scatter_done(line_send_f, rs_send_f, 0)
        pass_on().wait_send()

    scatter_done(line_send_b, rs_send_b, 1)

    @pl.when(t > 0)
    def _():
        pass_above().wait_send()

    pltpu.make_async_copy(final_recv, final_recv, final_sem.at[0]).wait()
    mine = lax.broadcasted_iota(jnp.int32, (ROWS, 1), 0) == lax.rem(r, ROWS)
    for j in range(4):
        rows = jnp.where(mine, final_recv[j].astype(F32), 0.0)
        grad_out[:, j * QUART : (j + 1) * QUART] = jnp.sum(rows, axis=0, keepdims=True).astype(BF)

    @pl.when(t == 0)
    def _():
        target, copy = final_above_copy()
        wait_sent(own_i, target, copy)

    @pl.when(is_final)
    def _():
        def one(n, carry):
            target, copy = final_copy(n)
            wait_sent(t, target, copy)
            return carry

        lax.fori_loop(0, ROWS, one, 0)


def body(tokens, cotangent, wiring, lengths, in_proj, out_proj, section_gain):
    vmem = pl.BlockSpec(memory_space=pltpu.VMEM)
    smem = pl.BlockSpec(memory_space=pltpu.SMEM)
    hbm = pl.BlockSpec(memory_space=pl.ANY)
    dma = pltpu.SemaphoreType.DMA
    normed, masked, pre_grad, act, grad = pl.pallas_call(
        kernel,
        name="relay",
        out_shape=(
            jax.ShapeDtypeStruct((CHUNKS, MICRO, ROWS, D), BF),
            jax.ShapeDtypeStruct((CHUNKS, MICRO, ROWS, D), BF),
            jax.ShapeDtypeStruct((CHUNKS, MICRO, ROWS, PIECE), BF),
            jax.ShapeDtypeStruct((CHUNKS, MICRO, ROWS, PIECE), BF),
            jax.ShapeDtypeStruct((1, D), BF),
        ),
        in_specs=[smem, smem, hbm, hbm, hbm, hbm, hbm],
        out_specs=(vmem,) * 5,
        scratch_shapes=[
            pltpu.VMEM((CHUNKS, MICRO, ROWS, D), BF),
            pltpu.VMEM((CHUNKS, MICRO, ROWS, D), BF),
            pltpu.VMEM((D, FF_DEV), BF),
            pltpu.VMEM((D, FF_DEV), BF),
            pltpu.VMEM((GROUPS, D), BF),
            pltpu.VMEM((GROUPS, D), F32),
            pltpu.VMEM((MICRO, D), BF),
            pltpu.VMEM((MICRO, 4, 1, QUART), F32),
            pltpu.VMEM((ROWS, 1, QUART), F32),
            pltpu.VMEM((CHUNKS, SLOT_ROWS, D), BF),
            pltpu.VMEM((CHUNKS, SLOT_ROWS, FF_DEV), F32),
            pltpu.VMEM((CHUNKS, SLOT_ROWS, 128), F32),
            pltpu.VMEM((CHUNKS, SLOT_ROWS, FF_DEV), BF),
            pltpu.VMEM((CHUNKS, SLOT_ROWS, FF_DEV), F32),
            pltpu.VMEM((GROUPS, CHUNKS, SLOT_ROWS, PIECE), BF),
            pltpu.VMEM((GROUPS, CHUNKS, SLOT_ROWS, PIECE), BF),
            pltpu.VMEM((GROUPS, CHUNKS, SLOT_ROWS, PIECE), BF),
            pltpu.VMEM((GROUPS, CHUNKS, SLOT_ROWS, PIECE), BF),
            pltpu.VMEM((CHUNKS, SLOT_ROWS, HALF), BF),
            pltpu.VMEM((SLOT_ROWS, HALF), BF),
            pltpu.VMEM((CHUNKS, SLOT_ROWS, HALF), BF),
            pltpu.VMEM((CHUNKS, 4, 2, ROWS, QUART), BF),
            pltpu.VMEM((CHUNKS, 4, 2, ROWS, QUART), BF),
            pltpu.VMEM((CHUNKS, 2, ROWS, QUART), BF),
            pltpu.VMEM((LINE, ROWS, QUART), BF),
            pltpu.VMEM((ROWS, QUART), BF),
            pltpu.VMEM((ROWS, QUART), BF),
            pltpu.VMEM((CHUNKS, SLOT_ROWS, HALF), BF),
            pltpu.VMEM((CHUNKS, SLOT_ROWS, HALF), BF),
            pltpu.VMEM((CHUNKS, 4, 2, ROWS, QUART), BF),
            pltpu.VMEM((CHUNKS, 4, 2, ROWS, QUART), BF),
            pltpu.VMEM((CHUNKS, 2, ROWS, QUART), BF),
            pltpu.VMEM((2, LINE, ROWS, QUART), BF),
            pltpu.VMEM((ROWS, QUART), BF),
            pltpu.VMEM((ROWS, QUART), BF),
            pltpu.VMEM((ROWS, QUART), BF),
            pltpu.VMEM((ROWS, QUART), BF),
            pltpu.VMEM((4, ROWS, QUART), BF),
            dma((4,)),
            pltpu.SemaphoreType.REGULAR,
            dma((1,)),
            dma((1,)),
            dma((CHUNKS,)),
            dma((CHUNKS,)),
            dma((CHUNKS,)),
            dma((CHUNKS,)),
            dma((1,)),
            dma((CHUNKS,)),
            dma((CHUNKS,)),
            dma((1,)),
            dma((2, CHUNKS)),
            dma((2,)),
            dma((3,)),
            dma((2,)),
            dma((2,)),
            dma((2,)),
            dma((2,)),
            dma((1,)),
            dma((1,)),
            dma((2, GROUPS)),
            dma((2, GROUPS)),
            dma((1,)),
            dma((1,)),
        ],
        compiler_params=pltpu.CompilerParams(
            collective_id=0, has_side_effects=True, vmem_limit_bytes=63 * 1024 * 1024
        ),
    )(wiring.transpose(0, 2, 1), lengths, tokens.reshape(MICRO, D), cotangent.reshape(MICRO, D), in_proj[0, 0], out_proj[0, 0], section_gain[0])
    column_block = pl.BlockSpec((CHUNKS, MICRO, ROWS, QUART), lambda n: (0, 0, 0, n))
    hidden_block = pl.BlockSpec((CHUNKS, MICRO, ROWS, PIECE), lambda n: (0, 0, 0, 0))
    out_block = pl.BlockSpec((PIECE, QUART), lambda n: (0, n))
    row_block = pl.BlockSpec((1, QUART), lambda n: (0, n))
    in_grad, out_grad, grad = pl.pallas_call(
        weight_kernel,
        name="weights",
        grid=(4,),
        out_shape=(
            jax.ShapeDtypeStruct((PIECE, D), BF),
            jax.ShapeDtypeStruct((PIECE, D), BF),
            jax.ShapeDtypeStruct((1, D), BF),
        ),
        in_specs=[column_block, hidden_block, column_block, hidden_block, row_block],
        out_specs=(out_block, out_block, row_block),
        compiler_params=pltpu.CompilerParams(vmem_limit_bytes=63 * 1024 * 1024),
    )(normed, pre_grad, masked, act, grad)
    return grad[None], in_grad.T[None], out_grad.T[None]


def weight_kernel(normed, pre_grad, masked, act, row, in_out, out_out, row_out):
    rows = CHUNKS * MICRO * ROWS
    for hidden, features, out in ((pre_grad, normed, in_out), (act, masked, out_out)):
        value = lax.dot_general(
            hidden[...].reshape(rows, PIECE), features[...].reshape(rows, QUART),
            (((0,), (0,)), ((), ())), preferred_element_type=F32,
        )
        out[...] = value.astype(BF)
    row_out[...] = row[...]


def solution(mesh):
    in_specs = (
        P(None, "replica", None),
        P(None, "replica", None),
        P(),
        P(),
        P("section", "replica", None, None),
        P("section", "replica", None, None),
        P("section", None, None),
    )
    out_specs = (
        P("section", "replica", None),
        P("section", None, "replica"),
        P("section", None, "replica"),
    )
    return jax.shard_map(body, mesh=mesh, in_specs=in_specs, out_specs=out_specs, check_vma=False)
```

```python
import jax
import jax.numpy as jnp
from jax import lax
from jax.experimental import pallas as pl
from jax.experimental.pallas import tpu as pltpu
from jax.sharding import PartitionSpec as P

D = 2560
FF_DEV = 640
GROUPS = 4
CAP = 2
MICRO = 4
CHUNKS = 4
ROWS = 16
HALF = D // 2
QUART = D // 4
SLOT_ROWS = CAP * ROWS
PIECE = FF_DEV // GROUPS
CHIPS = 32
LINE = 8
SPREAD_ORDER = sorted(
    ((dz, dy) for dz in range(8) for dy in range(4)),
    key=lambda shift: -(min(shift[0], 8 - shift[0]) + min(shift[1], 4 - shift[1])),
)

gelu_coeff = 0.7978845608028654
gelu_cubic = 0.044715
epsilon = 1e-05

BF = jnp.bfloat16
F32 = jnp.float32
NT = (((1,), (1,)), ((), ()))

def choose(index, values):
    picked = values[0]
    for n in range(1, len(values)):
        picked = jnp.where(index == n, values[n], picked)
    return picked


def norm_scale(rows):
    return lax.rsqrt(jnp.mean(rows * rows, axis=-1, keepdims=True) + epsilon)


def kernel(
    wiring, lengths, tokens, cotangent, w_in_hbm, w_out_hbm, gain_hbm,
    normed_out, masked_out, pre_out, act_out, grad_out,
    x_buf, u_buf, w_in, w_out, gain_rows, gains, entry_rows, entry_send, entry_recv,
    h_buf, pre_buf, inv_buf, act_buf, back_buf, pg_stage, act_stage, pg_all, act_all,
    merge_send_f, merge_own, merge_recv_f, line_send_f, line_recv_f, rs_send_f, rs_recv_f, own_f, held_recv,
    merge_send_b, merge_recv_b, line_send_b, line_recv_b, rs_send_b, rs_recv_b, own_b, above_recv,
    final_above, final_own, final_recv,
    load_sem, go_sem, entry_sem, entry_send_sem, x_sem, x_core_sem, u_sem, u_core_sem, core_send_sem,
    merge_sem_f, merge_sem_b, merge_send_sem, line_sem, line_send_sem, rs_sem, rs_send_sem, ag_send_sem,
    pass_sem, pass_send_sem, above_sem, above_send_sem, grads_sem, grads_send_sem, final_sem, final_send_sem,
):
    t = lax.axis_index("section")
    r = lax.axis_index("replica")
    core = lax.rem(r, 2)
    other = 1 - core
    chip = lax.div(r, 2)
    z = lax.div(r, 8)
    y = lax.rem(chip, 4)
    g = lax.rem(r, 4)
    part = lax.div(r, 4)
    last = lax.axis_size("section") - 1
    own_k = lax.rem(z + 2 * core, 4)
    own_i = 2 * lax.div(z, 4) + lax.rem(y, 2)
    own_j = 2 * core + lax.div(y, 2)
    own_cols = pl.ds(pl.multiple_of(own_j * QUART, 128), QUART)
    own_turn = jnp.maximum(own_k - 2, 0)
    mate = r + 1 - 2 * core
    my_half = pl.ds(pl.multiple_of(core * HALF, 128), HALF)
    mate_half = pl.ds(pl.multiple_of(other * HALF, 128), HALF)
    mate_rows = pl.ds(pl.multiple_of(other * HALF, HALF), HALF)
    my_rows = pl.ds(pl.multiple_of(core * HALF, HALF), HALF)

    routes = [wiring[t, 0, i] for i in range(MICRO)]
    lens = [lengths[i] for i in range(MICRO)]
    slots = []
    for i in range(MICRO):
        taken = jnp.int32(0)
        for e in range(i):
            taken = taken + jnp.where(routes[e] == routes[i], 1, 0)
        slots.append(taken)
    slot_mb, slot_len = [], []
    for c in range(CAP):
        number, length = jnp.int32(0), jnp.int32(0)
        for i in range(MICRO):
            here = (routes[i] == g) & (slots[i] == c)
            number = jnp.where(here, i, number)
            length = jnp.where(here, lens[i], length)
        slot_mb.append(number)
        slot_len.append(length)
    mate_g = g + 1 - 2 * core
    merge_from = [
        jnp.where(routes[i] == g, slots[i], jnp.where(routes[i] == mate_g, CAP + slots[i], 2 * CAP))
        for i in range(MICRO)
    ]

    def to(section, replica):
        return dict(device_id=(section, replica), device_id_type=pl.DeviceIdType.MESH)

    def start_or_keep(target_section, target, remote, source, dest, sem):
        here = (target == r) & (target_section == t)

        @pl.when(jnp.logical_not(here))
        def _():
            remote.start()

        @pl.when(here)
        def _():
            pltpu.make_async_copy(source, dest, sem).start()

    def wait_sent(target_section, target, remote):
        @pl.when(jnp.logical_not((target == r) & (target_section == t)))
        def _():
            remote.wait_send()

    def owner_z(k, oc):
        return lax.rem(k + 2 * oc, 4)

    entry_z = [owner_z(lax.div(r, ROWS), oc) for oc in range(2)]

    def entry_copy(n):
        i, j = n // 4, n % 4
        oy = 2 * (j % 2) + i % 2
        target = (entry_z[j // 2] + 4 * (i // 2)) * 8 + oy * 2 + j // 2
        source, dest = entry_send.at[i, j], entry_recv.at[lax.rem(r, ROWS)]
        return target, source, dest, pltpu.make_async_remote_copy(
            source, dest, entry_send_sem.at[0], entry_sem.at[0], **to(t, target)
        )

    in_load = pltpu.make_async_copy(w_in_hbm, w_in, load_sem.at[0])
    out_load = pltpu.make_async_copy(w_out_hbm, w_out, load_sem.at[1])
    gain_load = pltpu.make_async_copy(gain_hbm, gain_rows, load_sem.at[2])
    ends = (t == 0) | (t == last)

    @pl.when(t == 0)
    def _():
        pltpu.make_async_copy(tokens, entry_rows, load_sem.at[3]).start()

    @pl.when(t == last)
    def _():
        pltpu.make_async_copy(cotangent, entry_rows, load_sem.at[3]).start()

    gain_load.start()
    in_load.start()
    out_load.start()

    barrier = pltpu.get_barrier_semaphore()
    planes = lax.axis_size("section")
    replicas = lax.axis_size("replica")

    def tell_line(n, carry):
        for shift in (1, planes - 1):
            there = lax.rem(t + shift, planes)
            pl.semaphore_signal(barrier, inc=1, **to(there, n * 8 + y * 2 + other))
        return carry

    def tell_plane(n, carry):
        pl.semaphore_signal(barrier, inc=1, **to(t, lax.rem(r + n, replicas)))
        return carry

    lax.fori_loop(1, replicas, tell_plane, 0)
    lax.fori_loop(0, LINE, tell_line, 0)
    for shift in (1, planes - 1):
        pl.semaphore_signal(barrier, inc=1, **to(lax.rem(t + shift, planes), r))

    is_final = (lax.rem(y, 2) == lax.rem(t, 2)) & (lax.rem(z, 2) == lax.div(t, 2))
    final_k = lax.div(z, 2)
    final_j = 2 * core + lax.div(y, 2)

    @pl.when(t == 2)
    def _():
        def tell_first(n, carry):
            pl.semaphore_signal(barrier, inc=1, **to(0, n * 8 + y * 2 + other))
            return carry

        lax.fori_loop(0, LINE, tell_first, 0)

    @pl.when((t > 0) & is_final)
    def _():
        holder = (4 * lax.div(t, 2) + owner_z(final_k, core)) * 8 + y * 2 + core
        pl.semaphore_signal(barrier, inc=1, **to(0, holder))

    @pl.when(ends)
    def _():
        pltpu.make_async_copy(tokens, entry_rows, load_sem.at[3]).wait()
        for i in range(MICRO):
            row = entry_rows[i : i + 1, :].astype(F32)
            for j in range(4):
                entry_send[i, j] = row[:, j * QUART : (j + 1) * QUART]

    gain_load.wait()
    gains[...] = gain_rows[...].astype(F32)
    pl.semaphore_wait(barrier, replicas - 1 + 2 * LINE + 2 + jnp.where(t == 0, LINE + jnp.where(own_i > 0, 1, 0), 0))

    @pl.when(ends)
    def _():
        for n in range(MICRO * 4):
            target, source, dest, copy = entry_copy(n)
            start_or_keep(t, target, copy, source, dest, entry_sem.at[0])

    def entered():
        pltpu.make_async_copy(entry_recv, entry_recv, entry_sem.at[0]).wait()
        return entry_recv[...].reshape(ROWS, QUART).astype(BF)

    def gain_row(group):
        return choose(group, [gains[n : n + 1, :] for n in range(GROUPS)])

    def arrive(buf, k, sem, core_sem):
        view = buf.at[k, :, :, mate_half]
        pltpu.make_async_copy(view, view, sem.at[k]).wait()
        copy = pltpu.make_async_remote_copy(view, view, core_send_sem.at[0], core_sem.at[k], **to(t, mate))
        copy.start()
        return copy

    def slot_rows(buf, k, cols):
        rows = [buf[k, i, :, cols] for i in range(MICRO)]
        return jnp.concatenate([choose(slot_mb[c], rows) for c in range(CAP)], axis=0)

    def gain_part(cols):
        return choose(g, [gains[n : n + 1, cols] for n in range(GROUPS)])

    def slot_live(k):
        return jnp.concatenate([live_rows(k, slot_len[c]).astype(F32) for c in range(CAP)], axis=0)

    def x_stage(k):
        copy = arrive(x_buf, k, x_sem, x_core_sem)

        def half(cols, rows):
            held = slot_rows(x_buf, k, cols)
            h_buf[k, :, cols] = held
            flat = held.astype(F32)
            scaled = (flat * gain_part(cols)).astype(BF)
            squares = jnp.sum(flat * flat, axis=-1, keepdims=True)
            return squares, jnp.dot(scaled, w_in[rows, :], preferred_element_type=F32)

        mine = half(mate_half, mate_rows)
        copy.wait()
        theirs = half(my_half, my_rows)
        inv = lax.rsqrt((mine[0] + theirs[0]) * (1.0 / D) + epsilon)
        inv_buf[k] = jnp.broadcast_to(inv, (SLOT_ROWS, 128))
        pre = (mine[1] + theirs[1]) * inv
        pre_buf[k] = pre
        act = jax.nn.gelu(pre, approximate=True).astype(BF)
        act_buf[k] = act
        return act

    def u_stage(k):
        copy = arrive(u_buf, k, u_sem, u_core_sem)
        live = slot_live(k)

        def half(cols, rows):
            masked = (slot_rows(u_buf, k, cols).astype(F32) * live).astype(BF)
            return jnp.dot(masked, w_out[rows, :], preferred_element_type=F32)

        mine = half(mate_half, mate_rows)
        copy.wait()
        back_buf[k] = mine + half(my_half, my_rows)

    def merge_copy(k, send, recv, sem):
        return pltpu.make_async_remote_copy(
            send.at[k], recv.at[k], merge_send_sem.at[0], sem.at[k], **to(t, mate)
        )

    line_base = z * 8 + other

    def scatter(k, half, send, recv, line_send, line_recv, sem, way):
        send[k] = half(mate_rows, mate_half)
        copy = merge_copy(k, send, recv, sem)
        copy.start()
        merge_own[...] = half(my_rows, my_half)
        copy.wait()
        for i in range(MICRO):
            merged = choose(
                merge_from[i],
                [
                    merge_own[0:ROWS, :], merge_own[ROWS:SLOT_ROWS, :],
                    recv[k, 0:ROWS, :], recv[k, ROWS:SLOT_ROWS, :], jnp.zeros((ROWS, HALF), BF),
                ],
            )
            for jj in range(2):
                line_send[k, 2 * jj + i % 2, i // 2] = merged[:, jj * QUART : (jj + 1) * QUART]
        for dy in (2, 1, 3, 0):
            there = lax.rem(y + dy, 4)
            pltpu.make_async_remote_copy(
                line_send.at[k, there], line_recv.at[k, y], line_send_sem.at[way], line_sem.at[way, k],
                **to(t, line_base + 2 * there),
            ).start()

    def relay(k, target, line_recv, rs_send, rs_recv, way, slot):
        pltpu.make_async_copy(line_recv.at[k], line_recv.at[k], line_sem.at[way, k]).wait()
        for n in range(2):
            section, there = target(k, n)
            pieces = [line_recv[k, e, n].astype(F32) for e in range(4)]
            rs_send[k, n] = ((pieces[0] + pieces[1]) + (pieces[2] + pieces[3])).astype(BF)
            pltpu.make_async_remote_copy(
                rs_send.at[k, n], rs_recv.at[z], rs_send_sem.at[way], rs_sem.at[slot],
                **to(section, there),
            ).start()

    def forward_target(k, n):
        return t + 1, (owner_z(k, other) + 4 * n) * 8 + y * 2 + other

    def backward_target(k, n):
        section = jnp.where(t == 0, 2 * n + lax.rem(y, 2), t - 1)
        line = jnp.where(t == 0, 2 * k + n, owner_z(k, other) + 4 * n)
        return section, line * 8 + y * 2 + other

    def relay_turn(k, target, line_recv, rs_send, rs_recv, way, slot):
        @pl.when(k > 0)
        def _():
            relay(k - 1, target, line_recv, rs_send, rs_recv, way, slot)

        @pl.when(k == CHUNKS - 1)
        def _():
            relay(k, target, line_recv, rs_send, rs_recv, way, slot)

    def scatter_done(line_send, rs_send, way):
        pltpu.make_async_copy(line_send, line_send, line_send_sem.at[way]).wait()
        pltpu.make_async_copy(rs_send, rs_send, rs_send_sem.at[way]).wait()

    def live_rows(k, length):
        position = k * ROWS + lax.broadcasted_iota(jnp.int32, (ROWS, 1), 0)
        return position < length

    spread_z = [lax.rem(z + dz, 8) * 8 + other for dz in range(8)]
    spread_y = [lax.rem(y + dy, 4) * 2 for dy in range(4)]

    def spread(source, buf, sem, way):
        for dz, dy in SPREAD_ORDER:
            pltpu.make_async_remote_copy(
                source, buf.at[own_k, own_i, :, own_cols], ag_send_sem.at[way], sem.at[own_k],
                **to(t, spread_z[dz] + spread_y[dy]),
            ).start()

    def spread_done(source, way):
        def one(n, carry):
            pltpu.make_async_copy(source, source, ag_send_sem.at[way]).wait()
            return carry

        lax.fori_loop(0, CHIPS, one, 0)

    def pass_copy(source, dest, section, way):
        return pltpu.make_async_remote_copy(
            source, dest, pass_send_sem.at[way], pass_sem.at[way], **to(section, r)
        )

    def pass_on():
        return pass_copy(own_f, held_recv, t + 1, 0)

    def final_above_copy():
        target = (2 * own_k + lax.div(own_i, 2)) * 8 + y * 2 + core
        return target, pltpu.make_async_remote_copy(
            own_b, final_above, above_send_sem.at[0], above_sem.at[0], **to(own_i, target)
        )

    def pass_above():
        return pass_copy(own_b, above_recv, t - 1, 1)

    def received(dest, way):
        pltpu.make_async_copy(dest, dest, pass_sem.at[way]).wait()

    def combined(before, pieces, slot):
        pltpu.make_async_copy(pieces, pieces, rs_sem.at[slot]).wait()
        return (before.astype(F32) + jnp.sum(pieces[...].astype(F32), axis=0)).astype(BF)

    def own_forward():
        @pl.when(t == 0)
        def _():
            own_f[...] = entered()

            @pl.when(own_k > 0)
            def _():
                pl.semaphore_wait(go_sem, 1)

        @pl.when(t > 0)
        def _():
            received(held_recv, 0)
            own_f[...] = combined(held_recv[...], rs_recv_f, 0)

        spread(own_f, x_buf, x_sem, 0)

        @pl.when((t == 0) & (own_k < CHUNKS - 1))
        def _():
            pl.semaphore_signal(go_sem, inc=1, **to(t, lax.rem(r + 8, replicas)))

        @pl.when(t < last)
        def _():
            pass_on().start()


    def own_backward():
        @pl.when(t == last)
        def _():
            own_b[...] = entered()

        @pl.when(t < last)
        def _():
            received(above_recv, 1)
            own_b[...] = combined(above_recv[...], rs_recv_b.at[0], 1)

        spread(own_b, u_buf, u_sem, 1)

        @pl.when(t > 0)
        def _():
            pass_above().start()

        @pl.when(t == 0)
        def _():
            target, copy = final_above_copy()
            start_or_keep(own_i, target, copy, own_b, final_above, above_sem.at[0])

    def gather_normed(k, carry):
        for i in range(MICRO):
            rows = x_buf[k, i].astype(F32)
            gain = gain_row(routes[i])
            normed_out[k, i] = (rows * norm_scale(rows) * gain).astype(BF)
        return carry

    def gather_masked(k, carry):
        for i in range(MICRO):
            live = live_rows(k, lens[i]).astype(F32)
            masked_out[k, i] = (u_buf[k, i].astype(F32) * live).astype(BF)
        return carry

    def grads_copy(d, stage, gathered, which):
        there = lax.rem(g + d, GROUPS)
        return pltpu.make_async_remote_copy(
            stage.at[there], gathered.at[g], grads_send_sem.at[which, d], grads_sem.at[which, d],
            **to(t, part * GROUPS + there),
        )

    def send_act():
        for d in range(1, GROUPS):
            grads_copy(d, act_stage, act_all, 1).start()

    def split_act(k, carry):
        for n in range(GROUPS):
            act_stage[n, k] = act_buf[k, :, n * PIECE : (n + 1) * PIECE]
        return carry

    @pl.when(t == last)
    def _():
        own_backward()
        out_load.wait()

        def step(k, carry):
            u_stage(k)
            return carry

        lax.fori_loop(0, CHUNKS, step, 0)
        lax.fori_loop(0, CHUNKS, gather_masked, 0)
        in_load.wait()

    @pl.when(t < last)
    def _():
        in_load.wait()
        out_load.wait()

        def step(k, carry):
            @pl.when(k == own_turn)
            def _():
                own_forward()

            act = (x_stage(k).astype(F32) * slot_live(k)).astype(BF)

            def half(rows, cols):
                return lax.dot_general(act, w_out[rows, :], NT, preferred_element_type=F32).astype(BF)

            scatter(k, half, merge_send_f, merge_recv_f, line_send_f, line_recv_f, merge_sem_f, 0)
            relay_turn(k, forward_target, line_recv_f, rs_send_f, rs_recv_f, 0, 0)
            return carry

        lax.fori_loop(0, CHUNKS, step, 0)
        lax.fori_loop(0, CHUNKS, split_act, 0)
        send_act()
        lax.fori_loop(0, CHUNKS, gather_normed, 0)

    back_slot = jnp.where(t == 0, 1, 0)

    def back(k, carry):
        @pl.when((t == last) & (k == own_turn))
        def _():
            own_forward()

        @pl.when((t < last) & (k == own_turn))
        def _():
            own_backward()

        @pl.when(t == last)
        def _():
            x_stage(k)

        @pl.when(t < last)
        def _():
            u_stage(k)

        pre = pre_buf[k]
        inner = gelu_coeff * (pre + gelu_cubic * pre * pre * pre)
        tangent = jnp.tanh(inner)
        slope = 0.5 * (1.0 + tangent) + 0.5 * pre * (1.0 - tangent * tangent) * gelu_coeff * (
            1.0 + 3.0 * gelu_cubic * pre * pre
        )
        pre_grad = (back_buf[k] * slope).astype(BF)
        inv = inv_buf[k, :, 0:1]
        dots = jnp.sum(pre_grad.astype(F32) * pre, axis=-1, keepdims=True) * (inv * inv * (1.0 / D))

        def half(rows, cols):
            value = lax.dot_general(pre_grad, w_in[rows, :], NT, preferred_element_type=F32)
            return (value * inv * gain_part(cols) - h_buf[k, :, cols].astype(F32) * dots).astype(BF)

        scatter(k, half, merge_send_b, merge_recv_b, line_send_b, line_recv_b, merge_sem_b, 1)
        for n in range(GROUPS):
            pg_stage[n, k] = pre_grad[:, n * PIECE : (n + 1) * PIECE]
        relay_turn(k, backward_target, line_recv_b, rs_send_b, rs_recv_b.at[back_slot], 1, 1 + back_slot)
        return carry

    lax.fori_loop(0, CHUNKS, back, 0)

    for d in range(1, GROUPS):
        grads_copy(d, pg_stage, pg_all, 0).start()

    @pl.when(t == last)
    def _():
        lax.fori_loop(0, CHUNKS, split_act, 0)
        send_act()
        lax.fori_loop(0, CHUNKS, gather_normed, 0)

    @pl.when(t < last)
    def _():
        lax.fori_loop(0, CHUNKS, gather_masked, 0)

    pg_all[g] = pg_stage[g]
    act_all[g] = act_stage[g]

    def final_copy(n):
        target = final_k * ROWS + n
        return target, pltpu.make_async_remote_copy(
            final_own, final_recv.at[final_j], final_send_sem.at[0], final_sem.at[0], **to(t, target)
        )

    def send_final():
        pltpu.make_async_copy(final_above, final_above, above_sem.at[0]).wait()
        final_own[...] = combined(final_above[...], rs_recv_b.at[1], 2)

        def one(n, carry):
            target, copy = final_copy(n)
            start_or_keep(t, target, copy, final_own, final_recv.at[final_j], final_sem.at[0])
            return carry

        lax.fori_loop(0, ROWS, one, 0)

    for d in range(1, GROUPS):
        grads_copy(d, pg_stage, pg_all, 0).wait()
        grads_copy(d, act_stage, act_all, 1).wait()

    def gather_hidden(k, carry):
        for gathered, out in ((pg_all, pre_out), (act_all, act_out)):
            pieces = [
                gathered[n, k, c * ROWS : (c + 1) * ROWS, :] for n in range(GROUPS) for c in range(CAP)
            ]
            for i in range(MICRO):
                out[k, i] = choose(routes[i] * CAP + slots[i], pieces)
        return carry

    @pl.when(t > 0)
    def _():
        lax.fori_loop(0, CHUNKS, gather_hidden, 0)

    @pl.when(is_final)
    def _():
        send_final()

    @pl.when(t == 0)
    def _():
        lax.fori_loop(0, CHUNKS, gather_hidden, 0)

    @pl.when((t == 0) | (t == last))
    def _():
        for n in range(MICRO * 4):
            target, source, dest, copy = entry_copy(n)
            wait_sent(t, target, copy)

    spread_done(own_f, 0)
    spread_done(own_b, 1)

    @pl.when(t < last)
    def _():
        scatter_done(line_send_f, rs_send_f, 0)
        pass_on().wait_send()

    scatter_done(line_send_b, rs_send_b, 1)

    @pl.when(t > 0)
    def _():
        pass_above().wait_send()

    pltpu.make_async_copy(final_recv, final_recv, final_sem.at[0]).wait()
    mine = lax.broadcasted_iota(jnp.int32, (ROWS, 1), 0) == lax.rem(r, ROWS)
    for j in range(4):
        rows = jnp.where(mine, final_recv[j].astype(F32), 0.0)
        grad_out[:, j * QUART : (j + 1) * QUART] = jnp.sum(rows, axis=0, keepdims=True).astype(BF)

    @pl.when(t == 0)
    def _():
        target, copy = final_above_copy()
        wait_sent(own_i, target, copy)

    @pl.when(is_final)
    def _():
        def one(n, carry):
            target, copy = final_copy(n)
            wait_sent(t, target, copy)
            return carry

        lax.fori_loop(0, ROWS, one, 0)


def body(tokens, cotangent, wiring, lengths, in_proj, out_proj, section_gain):
    vmem = pl.BlockSpec(memory_space=pltpu.VMEM)
    smem = pl.BlockSpec(memory_space=pltpu.SMEM)
    hbm = pl.BlockSpec(memory_space=pl.ANY)
    dma = pltpu.SemaphoreType.DMA
    normed, masked, pre_grad, act, grad = pl.pallas_call(
        kernel,
        name="relay",
        out_shape=(
            jax.ShapeDtypeStruct((CHUNKS, MICRO, ROWS, D), BF),
            jax.ShapeDtypeStruct((CHUNKS, MICRO, ROWS, D), BF),
            jax.ShapeDtypeStruct((CHUNKS, MICRO, ROWS, PIECE), BF),
            jax.ShapeDtypeStruct((CHUNKS, MICRO, ROWS, PIECE), BF),
            jax.ShapeDtypeStruct((1, D), BF),
        ),
        in_specs=[smem, smem, hbm, hbm, hbm, hbm, hbm],
        out_specs=(vmem,) * 5,
        scratch_shapes=[
            pltpu.VMEM((CHUNKS, MICRO, ROWS, D), BF),
            pltpu.VMEM((CHUNKS, MICRO, ROWS, D), BF),
            pltpu.VMEM((D, FF_DEV), BF),
            pltpu.VMEM((D, FF_DEV), BF),
            pltpu.VMEM((GROUPS, D), BF),
            pltpu.VMEM((GROUPS, D), F32),
            pltpu.VMEM((MICRO, D), BF),
            pltpu.VMEM((MICRO, 4, 1, QUART), F32),
            pltpu.VMEM((ROWS, 1, QUART), F32),
            pltpu.VMEM((CHUNKS, SLOT_ROWS, D), BF),
            pltpu.VMEM((CHUNKS, SLOT_ROWS, FF_DEV), F32),
            pltpu.VMEM((CHUNKS, SLOT_ROWS, 128), F32),
            pltpu.VMEM((CHUNKS, SLOT_ROWS, FF_DEV), BF),
            pltpu.VMEM((CHUNKS, SLOT_ROWS, FF_DEV), F32),
            pltpu.VMEM((GROUPS, CHUNKS, SLOT_ROWS, PIECE), BF),
            pltpu.VMEM((GROUPS, CHUNKS, SLOT_ROWS, PIECE), BF),
            pltpu.VMEM((GROUPS, CHUNKS, SLOT_ROWS, PIECE), BF),
            pltpu.VMEM((GROUPS, CHUNKS, SLOT_ROWS, PIECE), BF),
            pltpu.VMEM((CHUNKS, SLOT_ROWS, HALF), BF),
            pltpu.VMEM((SLOT_ROWS, HALF), BF),
            pltpu.VMEM((CHUNKS, SLOT_ROWS, HALF), BF),
            pltpu.VMEM((CHUNKS, 4, 2, ROWS, QUART), BF),
            pltpu.VMEM((CHUNKS, 4, 2, ROWS, QUART), BF),
            pltpu.VMEM((CHUNKS, 2, ROWS, QUART), BF),
            pltpu.VMEM((LINE, ROWS, QUART), BF),
            pltpu.VMEM((ROWS, QUART), BF),
            pltpu.VMEM((ROWS, QUART), BF),
            pltpu.VMEM((CHUNKS, SLOT_ROWS, HALF), BF),
            pltpu.VMEM((CHUNKS, SLOT_ROWS, HALF), BF),
            pltpu.VMEM((CHUNKS, 4, 2, ROWS, QUART), BF),
            pltpu.VMEM((CHUNKS, 4, 2, ROWS, QUART), BF),
            pltpu.VMEM((CHUNKS, 2, ROWS, QUART), BF),
            pltpu.VMEM((2, LINE, ROWS, QUART), BF),
            pltpu.VMEM((ROWS, QUART), BF),
            pltpu.VMEM((ROWS, QUART), BF),
            pltpu.VMEM((ROWS, QUART), BF),
            pltpu.VMEM((ROWS, QUART), BF),
            pltpu.VMEM((4, ROWS, QUART), BF),
            dma((4,)),
            pltpu.SemaphoreType.REGULAR,
            dma((1,)),
            dma((1,)),
            dma((CHUNKS,)),
            dma((CHUNKS,)),
            dma((CHUNKS,)),
            dma((CHUNKS,)),
            dma((1,)),
            dma((CHUNKS,)),
            dma((CHUNKS,)),
            dma((1,)),
            dma((2, CHUNKS)),
            dma((2,)),
            dma((3,)),
            dma((2,)),
            dma((2,)),
            dma((2,)),
            dma((2,)),
            dma((1,)),
            dma((1,)),
            dma((2, GROUPS)),
            dma((2, GROUPS)),
            dma((1,)),
            dma((1,)),
        ],
        compiler_params=pltpu.CompilerParams(
            collective_id=0, has_side_effects=True, vmem_limit_bytes=63 * 1024 * 1024
        ),
    )(wiring.transpose(0, 2, 1), lengths, tokens.reshape(MICRO, D), cotangent.reshape(MICRO, D), in_proj[0, 0], out_proj[0, 0], section_gain[0])
    column_block = pl.BlockSpec((CHUNKS, MICRO, ROWS, HALF), lambda n: (0, 0, 0, n))
    hidden_block = pl.BlockSpec((CHUNKS, MICRO, ROWS, PIECE), lambda n: (0, 0, 0, 0))
    out_block = pl.BlockSpec((PIECE, HALF), lambda n: (0, n))
    row_block = pl.BlockSpec((1, HALF), lambda n: (0, n))
    in_grad, out_grad, grad = pl.pallas_call(
        weight_kernel,
        name="weights",
        grid=(2,),
        out_shape=(
            jax.ShapeDtypeStruct((PIECE, D), BF),
            jax.ShapeDtypeStruct((PIECE, D), BF),
            jax.ShapeDtypeStruct((1, D), BF),
        ),
        in_specs=[column_block, hidden_block, column_block, hidden_block, row_block],
        out_specs=(out_block, out_block, row_block),
        compiler_params=pltpu.CompilerParams(vmem_limit_bytes=63 * 1024 * 1024),
    )(normed, pre_grad, masked, act, grad)
    return grad[None], in_grad.T[None], out_grad.T[None]


def weight_kernel(normed, pre_grad, masked, act, row, in_out, out_out, row_out):
    rows = CHUNKS * MICRO * ROWS
    for hidden, features, out in ((pre_grad, normed, in_out), (act, masked, out_out)):
        value = lax.dot_general(
            hidden[...].reshape(rows, PIECE), features[...].reshape(rows, HALF),
            (((0,), (0,)), ((), ())), preferred_element_type=F32,
        )
        out[...] = value.astype(BF)
    row_out[...] = row[...]


def solution(mesh):
    in_specs = (
        P(None, "replica", None),
        P(None, "replica", None),
        P(),
        P(),
        P("section", "replica", None, None),
        P("section", "replica", None, None),
        P("section", None, None),
    )
    out_specs = (
        P("section", "replica", None),
        P("section", None, "replica"),
        P("section", None, "replica"),
    )
    return jax.shard_map(body, mesh=mesh, in_specs=in_specs, out_specs=out_specs, check_vma=False)
```

```python
import jax
import jax.numpy as jnp
from jax import lax
from jax.experimental import pallas as pl
from jax.experimental.pallas import tpu as pltpu
from jax.sharding import PartitionSpec as P

D = 2560
FF_DEV = 640
GROUPS = 4
CAP = 2
MICRO = 4
CHUNKS = 4
ROWS = 16
HALF = D // 2
QUART = D // 4
SLOT_ROWS = CAP * ROWS
PIECE = FF_DEV // GROUPS
CHIPS = 32
LINE = 8
SPREAD_ORDER = sorted(
    ((dz, dy) for dz in range(8) for dy in range(4)),
    key=lambda shift: -(min(shift[0], 8 - shift[0]) + min(shift[1], 4 - shift[1])),
)

gelu_coeff = 0.7978845608028654
gelu_cubic = 0.044715
epsilon = 1e-05

BF = jnp.bfloat16
F32 = jnp.float32
NT = (((1,), (1,)), ((), ()))

def choose(index, values):
    picked = values[0]
    for n in range(1, len(values)):
        picked = jnp.where(index == n, values[n], picked)
    return picked


def norm_scale(rows):
    return lax.rsqrt(jnp.mean(rows * rows, axis=-1, keepdims=True) + epsilon)


def kernel(
    wiring, lengths, tokens, cotangent, w_in_hbm, w_out_hbm, gain_hbm,
    normed_out, masked_out, pre_out, act_out, grad_out,
    x_buf, u_buf, w_in, w_out, gain_rows, gains, entry_rows, entry_send, entry_recv,
    h_buf, pre_buf, inv_buf, act_buf, back_buf, pg_stage, act_stage, pg_all, act_all,
    merge_send_f, merge_own, merge_recv_f, line_send_f, line_recv_f, rs_send_f, rs_recv_f, own_f, held_recv,
    merge_send_b, merge_recv_b, line_send_b, line_recv_b, rs_send_b, rs_recv_b, own_b, above_recv,
    final_above, final_own, final_recv,
    load_sem, go_sem, entry_sem, entry_send_sem, x_sem, x_core_sem, u_sem, u_core_sem, core_send_sem,
    merge_sem_f, merge_sem_b, merge_send_sem, line_sem, line_send_sem, rs_sem, rs_send_sem, ag_send_sem,
    pass_sem, pass_send_sem, above_sem, above_send_sem, grads_sem, grads_send_sem, final_sem, final_send_sem,
):
    t = lax.axis_index("section")
    r = lax.axis_index("replica")
    core = lax.rem(r, 2)
    other = 1 - core
    chip = lax.div(r, 2)
    z = lax.div(r, 8)
    y = lax.rem(chip, 4)
    g = lax.rem(r, 4)
    part = lax.div(r, 4)
    last = lax.axis_size("section") - 1
    own_k = lax.rem(z + 2 * core, 4)
    own_i = 2 * lax.div(z, 4) + lax.rem(y, 2)
    own_j = 2 * core + lax.div(y, 2)
    own_cols = pl.ds(pl.multiple_of(own_j * QUART, 128), QUART)
    own_turn = jnp.maximum(own_k - 2, 0)
    mate = r + 1 - 2 * core
    my_half = pl.ds(pl.multiple_of(core * HALF, 128), HALF)
    mate_half = pl.ds(pl.multiple_of(other * HALF, 128), HALF)
    mate_rows = pl.ds(pl.multiple_of(other * HALF, HALF), HALF)
    my_rows = pl.ds(pl.multiple_of(core * HALF, HALF), HALF)

    routes = [wiring[t, 0, i] for i in range(MICRO)]
    lens = [lengths[i] for i in range(MICRO)]
    slots = []
    for i in range(MICRO):
        taken = jnp.int32(0)
        for e in range(i):
            taken = taken + jnp.where(routes[e] == routes[i], 1, 0)
        slots.append(taken)
    slot_mb, slot_len = [], []
    for c in range(CAP):
        number, length = jnp.int32(0), jnp.int32(0)
        for i in range(MICRO):
            here = (routes[i] == g) & (slots[i] == c)
            number = jnp.where(here, i, number)
            length = jnp.where(here, lens[i], length)
        slot_mb.append(number)
        slot_len.append(length)
    mate_g = g + 1 - 2 * core
    merge_from = [
        jnp.where(routes[i] == g, slots[i], jnp.where(routes[i] == mate_g, CAP + slots[i], 2 * CAP))
        for i in range(MICRO)
    ]

    def to(section, replica):
        return dict(device_id=(section, replica), device_id_type=pl.DeviceIdType.MESH)

    def start_or_keep(target_section, target, remote, source, dest, sem):
        here = (target == r) & (target_section == t)

        @pl.when(jnp.logical_not(here))
        def _():
            remote.start()

        @pl.when(here)
        def _():
            pltpu.make_async_copy(source, dest, sem).start()

    def wait_sent(target_section, target, remote):
        @pl.when(jnp.logical_not((target == r) & (target_section == t)))
        def _():
            remote.wait_send()

    def owner_z(k, oc):
        return lax.rem(k + 2 * oc, 4)

    entry_z = [owner_z(lax.div(r, ROWS), oc) for oc in range(2)]

    def entry_copy(n):
        i, j = n // 4, n % 4
        oy = 2 * (j % 2) + i % 2
        target = (entry_z[j // 2] + 4 * (i // 2)) * 8 + oy * 2 + j // 2
        source, dest = entry_send.at[i, j], entry_recv.at[lax.rem(r, ROWS)]
        return target, source, dest, pltpu.make_async_remote_copy(
            source, dest, entry_send_sem.at[0], entry_sem.at[0], **to(t, target)
        )

    in_load = pltpu.make_async_copy(w_in_hbm, w_in, load_sem.at[0])
    out_load = pltpu.make_async_copy(w_out_hbm, w_out, load_sem.at[1])
    gain_load = pltpu.make_async_copy(gain_hbm, gain_rows, load_sem.at[2])
    ends = (t == 0) | (t == last)

    @pl.when(t == 0)
    def _():
        pltpu.make_async_copy(tokens, entry_rows, load_sem.at[3]).start()

    @pl.when(t == last)
    def _():
        pltpu.make_async_copy(cotangent, entry_rows, load_sem.at[3]).start()

    gain_load.start()
    in_load.start()
    out_load.start()

    barrier = pltpu.get_barrier_semaphore()
    planes = lax.axis_size("section")
    replicas = lax.axis_size("replica")

    def tell_line(n, carry):
        for shift in (1, planes - 1):
            there = lax.rem(t + shift, planes)
            pl.semaphore_signal(barrier, inc=1, **to(there, n * 8 + y * 2 + other))
        return carry

    def tell_plane(n, carry):
        pl.semaphore_signal(barrier, inc=1, **to(t, lax.rem(r + n, replicas)))
        return carry

    lax.fori_loop(1, replicas, tell_plane, 0)
    lax.fori_loop(0, LINE, tell_line, 0)
    for shift in (1, planes - 1):
        pl.semaphore_signal(barrier, inc=1, **to(lax.rem(t + shift, planes), r))

    is_final = (lax.rem(y, 2) == lax.rem(t, 2)) & (lax.rem(z, 2) == lax.div(t, 2))
    final_k = lax.div(z, 2)
    final_j = 2 * core + lax.div(y, 2)

    @pl.when(t == 2)
    def _():
        def tell_first(n, carry):
            pl.semaphore_signal(barrier, inc=1, **to(0, n * 8 + y * 2 + other))
            return carry

        lax.fori_loop(0, LINE, tell_first, 0)

    @pl.when((t > 0) & is_final)
    def _():
        holder = (4 * lax.div(t, 2) + owner_z(final_k, core)) * 8 + y * 2 + core
        pl.semaphore_signal(barrier, inc=1, **to(0, holder))

    @pl.when(ends)
    def _():
        pltpu.make_async_copy(tokens, entry_rows, load_sem.at[3]).wait()
        for i in range(MICRO):
            row = entry_rows[i : i + 1, :].astype(F32)
            for j in range(4):
                entry_send[i, j] = row[:, j * QUART : (j + 1) * QUART]

    gain_load.wait()
    gains[...] = gain_rows[...].astype(F32)
    pl.semaphore_wait(barrier, replicas - 1 + 2 * LINE + 2 + jnp.where(t == 0, LINE + jnp.where(own_i > 0, 1, 0), 0))

    @pl.when(ends)
    def _():
        for n in range(MICRO * 4):
            target, source, dest, copy = entry_copy(n)
            start_or_keep(t, target, copy, source, dest, entry_sem.at[0])

    def entered():
        pltpu.make_async_copy(entry_recv, entry_recv, entry_sem.at[0]).wait()
        return entry_recv[...].reshape(ROWS, QUART).astype(BF)

    def gain_row(group):
        return choose(group, [gains[n : n + 1, :] for n in range(GROUPS)])

    def arrive(buf, k, sem, core_sem):
        view = buf.at[k, :, :, mate_half]
        pltpu.make_async_copy(view, view, sem.at[k]).wait()
        copy = pltpu.make_async_remote_copy(view, view, core_send_sem.at[0], core_sem.at[k], **to(t, mate))
        copy.start()
        return copy

    def slot_rows(buf, k, cols):
        rows = [buf[k, i, :, cols] for i in range(MICRO)]
        return jnp.concatenate([choose(slot_mb[c], rows) for c in range(CAP)], axis=0)

    def gain_part(cols):
        return choose(g, [gains[n : n + 1, cols] for n in range(GROUPS)])

    def slot_live(k):
        return jnp.concatenate([live_rows(k, slot_len[c]).astype(F32) for c in range(CAP)], axis=0)

    def x_stage(k):
        copy = arrive(x_buf, k, x_sem, x_core_sem)

        def half(cols, rows):
            held = slot_rows(x_buf, k, cols)
            h_buf[k, :, cols] = held
            flat = held.astype(F32)
            scaled = (flat * gain_part(cols)).astype(BF)
            squares = jnp.sum(flat * flat, axis=-1, keepdims=True)
            return squares, jnp.dot(scaled, w_in[rows, :], preferred_element_type=F32)

        mine = half(mate_half, mate_rows)
        copy.wait()
        theirs = half(my_half, my_rows)
        inv = lax.rsqrt((mine[0] + theirs[0]) * (1.0 / D) + epsilon)
        inv_buf[k] = jnp.broadcast_to(inv, (SLOT_ROWS, 128))
        pre = (mine[1] + theirs[1]) * inv
        pre_buf[k] = pre
        act = jax.nn.gelu(pre, approximate=True).astype(BF)
        act_buf[k] = act
        return act

    def u_stage(k):
        copy = arrive(u_buf, k, u_sem, u_core_sem)
        live = slot_live(k)

        def half(cols, rows):
            masked = (slot_rows(u_buf, k, cols).astype(F32) * live).astype(BF)
            return jnp.dot(masked, w_out[rows, :], preferred_element_type=F32)

        mine = half(mate_half, mate_rows)
        copy.wait()
        back_buf[k] = mine + half(my_half, my_rows)

    def merge_copy(k, send, recv, sem):
        return pltpu.make_async_remote_copy(
            send.at[k], recv.at[k], merge_send_sem.at[0], sem.at[k], **to(t, mate)
        )

    line_base = z * 8 + other

    def scatter(k, half, send, recv, line_send, line_recv, sem, way):
        send[k] = half(mate_rows, mate_half)
        copy = merge_copy(k, send, recv, sem)
        copy.start()
        merge_own[...] = half(my_rows, my_half)
        copy.wait()
        for i in range(MICRO):
            merged = choose(
                merge_from[i],
                [
                    merge_own[0:ROWS, :], merge_own[ROWS:SLOT_ROWS, :],
                    recv[k, 0:ROWS, :], recv[k, ROWS:SLOT_ROWS, :], jnp.zeros((ROWS, HALF), BF),
                ],
            )
            for jj in range(2):
                line_send[k, 2 * jj + i % 2, i // 2] = merged[:, jj * QUART : (jj + 1) * QUART]
        for dy in (2, 1, 3, 0):
            there = lax.rem(y + dy, 4)
            pltpu.make_async_remote_copy(
                line_send.at[k, there], line_recv.at[k, y], line_send_sem.at[way], line_sem.at[way, k],
                **to(t, line_base + 2 * there),
            ).start()

    def relay(k, target, line_recv, rs_send, rs_recv, way, slot):
        pltpu.make_async_copy(line_recv.at[k], line_recv.at[k], line_sem.at[way, k]).wait()
        for n in range(2):
            section, there = target(k, n)
            pieces = [line_recv[k, e, n].astype(F32) for e in range(4)]
            rs_send[k, n] = ((pieces[0] + pieces[1]) + (pieces[2] + pieces[3])).astype(BF)
            pltpu.make_async_remote_copy(
                rs_send.at[k, n], rs_recv.at[z], rs_send_sem.at[way], rs_sem.at[slot],
                **to(section, there),
            ).start()

    def forward_target(k, n):
        return t + 1, (owner_z(k, other) + 4 * n) * 8 + y * 2 + other

    def backward_target(k, n):
        section = jnp.where(t == 0, 2 * n + lax.rem(y, 2), t - 1)
        line = jnp.where(t == 0, 2 * k + n, owner_z(k, other) + 4 * n)
        return section, line * 8 + y * 2 + other

    def relay_turn(k, target, line_recv, rs_send, rs_recv, way, slot):
        @pl.when(k > 0)
        def _():
            relay(k - 1, target, line_recv, rs_send, rs_recv, way, slot)

        @pl.when(k == CHUNKS - 1)
        def _():
            relay(k, target, line_recv, rs_send, rs_recv, way, slot)

    def scatter_done(line_send, rs_send, way):
        pltpu.make_async_copy(line_send, line_send, line_send_sem.at[way]).wait()
        pltpu.make_async_copy(rs_send, rs_send, rs_send_sem.at[way]).wait()

    def live_rows(k, length):
        position = k * ROWS + lax.broadcasted_iota(jnp.int32, (ROWS, 1), 0)
        return position < length

    spread_z = [lax.rem(z + dz, 8) * 8 + other for dz in range(8)]
    spread_y = [lax.rem(y + dy, 4) * 2 for dy in range(4)]

    def spread(source, buf, sem, way):
        for dz, dy in SPREAD_ORDER:
            pltpu.make_async_remote_copy(
                source, buf.at[own_k, own_i, :, own_cols], ag_send_sem.at[way], sem.at[own_k],
                **to(t, spread_z[dz] + spread_y[dy]),
            ).start()

    def spread_done(source, way):
        def one(n, carry):
            pltpu.make_async_copy(source, source, ag_send_sem.at[way]).wait()
            return carry

        lax.fori_loop(0, CHIPS, one, 0)

    def pass_copy(source, dest, section, way):
        return pltpu.make_async_remote_copy(
            source, dest, pass_send_sem.at[way], pass_sem.at[way], **to(section, r)
        )

    def pass_on():
        return pass_copy(own_f, held_recv, t + 1, 0)

    def final_above_copy():
        target = (2 * own_k + lax.div(own_i, 2)) * 8 + y * 2 + core
        return target, pltpu.make_async_remote_copy(
            own_b, final_above, above_send_sem.at[0], above_sem.at[0], **to(own_i, target)
        )

    def pass_above():
        return pass_copy(own_b, above_recv, t - 1, 1)

    def received(dest, way):
        pltpu.make_async_copy(dest, dest, pass_sem.at[way]).wait()

    def combined(before, pieces, slot):
        pltpu.make_async_copy(pieces, pieces, rs_sem.at[slot]).wait()
        return (before.astype(F32) + jnp.sum(pieces[...].astype(F32), axis=0)).astype(BF)

    def own_forward():
        @pl.when(t == 0)
        def _():
            own_f[...] = entered()

            @pl.when(own_k > 0)
            def _():
                pl.semaphore_wait(go_sem, 1)

        @pl.when(t > 0)
        def _():
            received(held_recv, 0)
            own_f[...] = combined(held_recv[...], rs_recv_f, 0)

        spread(own_f, x_buf, x_sem, 0)

        @pl.when((t == 0) & (own_k < CHUNKS - 1))
        def _():
            pl.semaphore_signal(go_sem, inc=1, **to(t, lax.rem(r + 8, replicas)))

        @pl.when(t < last)
        def _():
            pass_on().start()


    def own_backward():
        @pl.when(t == last)
        def _():
            own_b[...] = entered()

        @pl.when(t < last)
        def _():
            received(above_recv, 1)
            own_b[...] = combined(above_recv[...], rs_recv_b.at[0], 1)

        spread(own_b, u_buf, u_sem, 1)

        @pl.when(t > 0)
        def _():
            pass_above().start()

        @pl.when(t == 0)
        def _():
            target, copy = final_above_copy()
            start_or_keep(own_i, target, copy, own_b, final_above, above_sem.at[0])

    def gather_normed(k, carry):
        for i in range(MICRO):
            rows = x_buf[k, i].astype(F32)
            gain = gain_row(routes[i])
            normed_out[k, i] = (rows * norm_scale(rows) * gain).astype(BF)
        return carry

    def gather_masked(k, carry):
        for i in range(MICRO):
            live = live_rows(k, lens[i]).astype(F32)
            masked_out[k, i] = (u_buf[k, i].astype(F32) * live).astype(BF)
        return carry

    def grads_copy(d, stage, gathered, which):
        there = lax.rem(g + d, GROUPS)
        return pltpu.make_async_remote_copy(
            stage.at[there], gathered.at[g], grads_send_sem.at[which, d], grads_sem.at[which, d],
            **to(t, part * GROUPS + there),
        )

    def send_act():
        for d in range(1, GROUPS):
            grads_copy(d, act_stage, act_all, 1).start()

    def split_act(k, carry):
        for n in range(GROUPS):
            act_stage[n, k] = act_buf[k, :, n * PIECE : (n + 1) * PIECE]
        return carry

    @pl.when(t == last)
    def _():
        own_backward()
        out_load.wait()

        def step(k, carry):
            u_stage(k)
            return carry

        lax.fori_loop(0, CHUNKS, step, 0)
        lax.fori_loop(0, CHUNKS, gather_masked, 0)
        in_load.wait()

    @pl.when(t < last)
    def _():
        in_load.wait()
        out_load.wait()

        def step(k, carry):
            @pl.when(k == own_turn)
            def _():
                own_forward()

            act = (x_stage(k).astype(F32) * slot_live(k)).astype(BF)

            def half(rows, cols):
                return lax.dot_general(act, w_out[rows, :], NT, preferred_element_type=F32).astype(BF)

            scatter(k, half, merge_send_f, merge_recv_f, line_send_f, line_recv_f, merge_sem_f, 0)
            relay_turn(k, forward_target, line_recv_f, rs_send_f, rs_recv_f, 0, 0)
            return carry

        lax.fori_loop(0, CHUNKS, step, 0)
        lax.fori_loop(0, CHUNKS, split_act, 0)
        send_act()
        lax.fori_loop(0, CHUNKS, gather_normed, 0)

    back_slot = jnp.where(t == 0, 1, 0)

    def back(k, carry):
        @pl.when((t == last) & (k == own_turn))
        def _():
            own_forward()

        @pl.when((t < last) & (k == own_turn))
        def _():
            own_backward()

        @pl.when(t == last)
        def _():
            x_stage(k)

        @pl.when(t < last)
        def _():
            u_stage(k)

        pre = pre_buf[k]
        inner = gelu_coeff * (pre + gelu_cubic * pre * pre * pre)
        tangent = jnp.tanh(inner)
        slope = 0.5 * (1.0 + tangent) + 0.5 * pre * (1.0 - tangent * tangent) * gelu_coeff * (
            1.0 + 3.0 * gelu_cubic * pre * pre
        )
        pre_grad = (back_buf[k] * slope).astype(BF)
        inv = inv_buf[k, :, 0:1]
        dots = jnp.sum(pre_grad.astype(F32) * pre, axis=-1, keepdims=True) * (inv * inv * (1.0 / D))

        def half(rows, cols):
            value = lax.dot_general(pre_grad, w_in[rows, :], NT, preferred_element_type=F32)
            return (value * inv * gain_part(cols) - h_buf[k, :, cols].astype(F32) * dots).astype(BF)

        scatter(k, half, merge_send_b, merge_recv_b, line_send_b, line_recv_b, merge_sem_b, 1)
        for n in range(GROUPS):
            pg_stage[n, k] = pre_grad[:, n * PIECE : (n + 1) * PIECE]
        relay_turn(k, backward_target, line_recv_b, rs_send_b, rs_recv_b.at[back_slot], 1, 1 + back_slot)
        return carry

    lax.fori_loop(0, CHUNKS, back, 0)

    for d in range(1, GROUPS):
        grads_copy(d, pg_stage, pg_all, 0).start()

    @pl.when(t == last)
    def _():
        lax.fori_loop(0, CHUNKS, split_act, 0)
        send_act()
        lax.fori_loop(0, CHUNKS, gather_normed, 0)

    @pl.when(t < last)
    def _():
        lax.fori_loop(0, CHUNKS, gather_masked, 0)

    pg_all[g] = pg_stage[g]
    act_all[g] = act_stage[g]

    def final_copy(n):
        target = final_k * ROWS + n
        return target, pltpu.make_async_remote_copy(
            final_own, final_recv.at[final_j], final_send_sem.at[0], final_sem.at[0], **to(t, target)
        )

    def send_final():
        pltpu.make_async_copy(final_above, final_above, above_sem.at[0]).wait()
        final_own[...] = combined(final_above[...], rs_recv_b.at[1], 2)

        def one(n, carry):
            target, copy = final_copy(n)
            start_or_keep(t, target, copy, final_own, final_recv.at[final_j], final_sem.at[0])
            return carry

        lax.fori_loop(0, ROWS, one, 0)

    for d in range(1, GROUPS):
        grads_copy(d, pg_stage, pg_all, 0).wait()
        grads_copy(d, act_stage, act_all, 1).wait()

    def gather_hidden(k, carry):
        for gathered, out in ((pg_all, pre_out), (act_all, act_out)):
            pieces = [
                gathered[n, k, c * ROWS : (c + 1) * ROWS, :] for n in range(GROUPS) for c in range(CAP)
            ]
            for i in range(MICRO):
                out[k, i] = choose(routes[i] * CAP + slots[i], pieces)
        return carry

    @pl.when(t > 0)
    def _():
        lax.fori_loop(0, CHUNKS, gather_hidden, 0)

    @pl.when(is_final)
    def _():
        send_final()

    @pl.when(t == 0)
    def _():
        lax.fori_loop(0, CHUNKS, gather_hidden, 0)

    @pl.when((t == 0) | (t == last))
    def _():
        for n in range(MICRO * 4):
            target, source, dest, copy = entry_copy(n)
            wait_sent(t, target, copy)

    spread_done(own_f, 0)
    spread_done(own_b, 1)

    @pl.when(t < last)
    def _():
        scatter_done(line_send_f, rs_send_f, 0)
        pass_on().wait_send()

    scatter_done(line_send_b, rs_send_b, 1)

    @pl.when(t > 0)
    def _():
        pass_above().wait_send()

    pltpu.make_async_copy(final_recv, final_recv, final_sem.at[0]).wait()
    mine = lax.broadcasted_iota(jnp.int32, (ROWS, 1), 0) == lax.rem(r, ROWS)
    for j in range(4):
        rows = jnp.where(mine, final_recv[j].astype(F32), 0.0)
        grad_out[:, j * QUART : (j + 1) * QUART] = jnp.sum(rows, axis=0, keepdims=True).astype(BF)

    @pl.when(t == 0)
    def _():
        target, copy = final_above_copy()
        wait_sent(own_i, target, copy)

    @pl.when(is_final)
    def _():
        def one(n, carry):
            target, copy = final_copy(n)
            wait_sent(t, target, copy)
            return carry

        lax.fori_loop(0, ROWS, one, 0)


def body(tokens, cotangent, wiring, lengths, in_proj, out_proj, section_gain):
    vmem = pl.BlockSpec(memory_space=pltpu.VMEM)
    smem = pl.BlockSpec(memory_space=pltpu.SMEM)
    hbm = pl.BlockSpec(memory_space=pl.ANY)
    dma = pltpu.SemaphoreType.DMA
    normed, masked, pre_grad, act, grad = pl.pallas_call(
        kernel,
        name="relay",
        out_shape=(
            jax.ShapeDtypeStruct((CHUNKS, MICRO, ROWS, D), BF),
            jax.ShapeDtypeStruct((CHUNKS, MICRO, ROWS, D), BF),
            jax.ShapeDtypeStruct((CHUNKS, MICRO, ROWS, PIECE), BF),
            jax.ShapeDtypeStruct((CHUNKS, MICRO, ROWS, PIECE), BF),
            jax.ShapeDtypeStruct((1, D), BF),
        ),
        in_specs=[smem, smem, hbm, hbm, hbm, hbm, hbm],
        out_specs=(vmem,) * 5,
        scratch_shapes=[
            pltpu.VMEM((CHUNKS, MICRO, ROWS, D), BF),
            pltpu.VMEM((CHUNKS, MICRO, ROWS, D), BF),
            pltpu.VMEM((D, FF_DEV), BF),
            pltpu.VMEM((D, FF_DEV), BF),
            pltpu.VMEM((GROUPS, D), BF),
            pltpu.VMEM((GROUPS, D), F32),
            pltpu.VMEM((MICRO, D), BF),
            pltpu.VMEM((MICRO, 4, 1, QUART), F32),
            pltpu.VMEM((ROWS, 1, QUART), F32),
            pltpu.VMEM((CHUNKS, SLOT_ROWS, D), BF),
            pltpu.VMEM((CHUNKS, SLOT_ROWS, FF_DEV), F32),
            pltpu.VMEM((CHUNKS, SLOT_ROWS, 128), F32),
            pltpu.VMEM((CHUNKS, SLOT_ROWS, FF_DEV), BF),
            pltpu.VMEM((CHUNKS, SLOT_ROWS, FF_DEV), F32),
            pltpu.VMEM((GROUPS, CHUNKS, SLOT_ROWS, PIECE), BF),
            pltpu.VMEM((GROUPS, CHUNKS, SLOT_ROWS, PIECE), BF),
            pltpu.VMEM((GROUPS, CHUNKS, SLOT_ROWS, PIECE), BF),
            pltpu.VMEM((GROUPS, CHUNKS, SLOT_ROWS, PIECE), BF),
            pltpu.VMEM((CHUNKS, SLOT_ROWS, HALF), BF),
            pltpu.VMEM((SLOT_ROWS, HALF), BF),
            pltpu.VMEM((CHUNKS, SLOT_ROWS, HALF), BF),
            pltpu.VMEM((CHUNKS, 4, 2, ROWS, QUART), BF),
            pltpu.VMEM((CHUNKS, 4, 2, ROWS, QUART), BF),
            pltpu.VMEM((CHUNKS, 2, ROWS, QUART), BF),
            pltpu.VMEM((LINE, ROWS, QUART), BF),
            pltpu.VMEM((ROWS, QUART), BF),
            pltpu.VMEM((ROWS, QUART), BF),
            pltpu.VMEM((CHUNKS, SLOT_ROWS, HALF), BF),
            pltpu.VMEM((CHUNKS, SLOT_ROWS, HALF), BF),
            pltpu.VMEM((CHUNKS, 4, 2, ROWS, QUART), BF),
            pltpu.VMEM((CHUNKS, 4, 2, ROWS, QUART), BF),
            pltpu.VMEM((CHUNKS, 2, ROWS, QUART), BF),
            pltpu.VMEM((2, LINE, ROWS, QUART), BF),
            pltpu.VMEM((ROWS, QUART), BF),
            pltpu.VMEM((ROWS, QUART), BF),
            pltpu.VMEM((ROWS, QUART), BF),
            pltpu.VMEM((ROWS, QUART), BF),
            pltpu.VMEM((4, ROWS, QUART), BF),
            dma((4,)),
            pltpu.SemaphoreType.REGULAR,
            dma((1,)),
            dma((1,)),
            dma((CHUNKS,)),
            dma((CHUNKS,)),
            dma((CHUNKS,)),
            dma((CHUNKS,)),
            dma((1,)),
            dma((CHUNKS,)),
            dma((CHUNKS,)),
            dma((1,)),
            dma((2, CHUNKS)),
            dma((2,)),
            dma((3,)),
            dma((2,)),
            dma((2,)),
            dma((2,)),
            dma((2,)),
            dma((1,)),
            dma((1,)),
            dma((2, GROUPS)),
            dma((2, GROUPS)),
            dma((1,)),
            dma((1,)),
        ],
        compiler_params=pltpu.CompilerParams(
            collective_id=0, has_side_effects=True, vmem_limit_bytes=63 * 1024 * 1024
        ),
    )(wiring.transpose(0, 2, 1), lengths, tokens.reshape(MICRO, D), cotangent.reshape(MICRO, D), in_proj[0, 0], out_proj[0, 0], section_gain[0])
    column_block = pl.BlockSpec((CHUNKS, MICRO, ROWS, HALF), lambda n: (0, 0, 0, n))
    hidden_block = pl.BlockSpec((CHUNKS, MICRO, ROWS, PIECE), lambda n: (0, 0, 0, 0))
    out_block = pl.BlockSpec((PIECE, HALF), lambda n: (0, n))
    row_block = pl.BlockSpec((1, HALF), lambda n: (0, n))
    in_grad, out_grad, grad = pl.pallas_call(
        weight_kernel,
        name="weights",
        grid=(2,),
        out_shape=(
            jax.ShapeDtypeStruct((PIECE, D), BF),
            jax.ShapeDtypeStruct((PIECE, D), BF),
            jax.ShapeDtypeStruct((1, D), BF),
        ),
        in_specs=[column_block, hidden_block, column_block, hidden_block, row_block],
        out_specs=(out_block, out_block, row_block),
        scratch_shapes=[pltpu.VMEM((2, PIECE, CHUNKS * MICRO * ROWS), BF)],
        compiler_params=pltpu.CompilerParams(vmem_limit_bytes=63 * 1024 * 1024),
    )(normed, pre_grad, masked, act, grad)
    return grad[None], in_grad.T[None], out_grad.T[None]


def weight_kernel(normed, pre_grad, masked, act, row, in_out, out_out, row_out, turned):
    rows = CHUNKS * MICRO * ROWS

    @pl.when(pl.program_id(0) == 0)
    def _():
        for n, hidden in enumerate((pre_grad, act)):
            turned[n] = hidden[...].reshape(rows, PIECE).astype(F32).T.astype(BF)

    for n, (features, out) in enumerate(((normed, in_out), (masked, out_out))):
        value = jnp.dot(turned[n], features[...].reshape(rows, HALF), preferred_element_type=F32)
        out[...] = value.astype(BF)
    row_out[...] = row[...]


def solution(mesh):
    in_specs = (
        P(None, "replica", None),
        P(None, "replica", None),
        P(),
        P(),
        P("section", "replica", None, None),
        P("section", "replica", None, None),
        P("section", None, None),
    )
    out_specs = (
        P("section", "replica", None),
        P("section", None, "replica"),
        P("section", None, "replica"),
    )
    return jax.shard_map(body, mesh=mesh, in_specs=in_specs, out_specs=out_specs, check_vma=False)
```
